512 devices in a mesh: row: 16 (over x_lo, z), col: 32 (over y, x_hi, core).
Axes of the slice: x: 4 (x_hi: 2, x_lo: 2; x = x_hi * 2 + x_lo), y: 8, z: 8, core: 2. Of those that a mesh axis runs over, the one named last changes fastest.
Arguments:
- features: bfloat16 [65536, 256], P(('col', 'row')), may hold values from -6 to 6
- weight: bfloat16 [256, 256], replicated, may hold values from -0.375 to 0.375
- block_values: bfloat16 [16, 32, 96, 128, 128], P('row', 'col'), may hold values from -0.09375 to 0.09375
- block_rows: int32 [16, 32, 96], P('row', 'col'), may hold values from 0 to 31, as said below
- block_cols: int32 [16, 32, 96], P('row', 'col'), may hold values from 0 to 15, as said below
- counts: int32 [16, 32], P('row', 'col'), may hold values from 12 to 96, as said below
- cotangent: bfloat16 [65536, 256], P(('row', 'col')), may hold values from -24 to 24
Outputs:
- activations: bfloat16 [65536, 256], P(('row', 'col'))
- feature_grad: bfloat16 [65536, 256], P(('col', 'row'))
- weight_grad: float32 [256, 256], replicated
The draws below stay inside these ranges and needn't reach their ends.
Inputs may be any that keep to these rules, and one draw needn't show every extreme that they name: block_rows and block_cols give each slot's block position within its tile; the 96 positions of one tile are all distinct. `block_cols`: see block_rows. `counts`: slots at and past a tile's count are not part of A. Tile (i, j) is full (96 live slots) exactly where j modulo 16 equals i; other tiles hold at most 48.
All inputs are finite; a program needn't handle non-finite values.
Results may differ from the reference program's by a relative error of at most 0.03.
Values may be sent and summed in bfloat16 or wider, within the bound.
No kernel may reach another device: no remote copies, remote signals or barrier semaphores. Data moves between devices by JAX's collectives and lax.ppermute only.
A program may use at most 64 MiB of HBM per device.

```python
import math
import jax
import jax.numpy as jnp
from jax import lax

F = 256
BLOCK = 128
NODES = 65536
ROW_TILES = 16
COL_TILES = 32
TILE_BR = 32
TILE_BC = 16
BLOCKS_TILE = 96


def block_positions(key):
    keys = jax.random.split(key, ROW_TILES * COL_TILES)
    places = jax.vmap(lambda single: jax.random.permutation(single, TILE_BR * TILE_BC)[:BLOCKS_TILE])(keys)
    return places.reshape(ROW_TILES, COL_TILES, BLOCKS_TILE).astype(jnp.int32)


def draw_block_rows(key, part):
    places = block_positions(key)
    return (places // TILE_BC).astype(jnp.int32)


def draw_block_cols(key, part):
    places = block_positions(key)
    return (places % TILE_BC).astype(jnp.int32)


def draw_counts(key, part):
    key = jax.random.fold_in(key, 3)
    drawn = jax.random.randint(key, (ROW_TILES, COL_TILES), BLOCKS_TILE // 8, BLOCKS_TILE // 2 + 1)
    row_ids = jnp.arange(ROW_TILES)[:, None]
    col_ids = jnp.arange(COL_TILES)[None, :]
    return jnp.where(col_ids % ROW_TILES == row_ids, BLOCKS_TILE, drawn).astype(jnp.int32)


def with_spikes(values, own_key, source, target, blocks, factor):
    def block_of(position):
        return (jnp.arange(values.shape[position]) // (values.shape[position] // blocks)).reshape((-1,) + (1,) * (values.ndim - 1 - position))

    one_side = jax.random.permutation(own_key, blocks)[block_of(target)]
    other_side = (block_of(target) + blocks // 2) % blocks
    return jnp.where((block_of(source) == one_side) | (block_of(source) == other_side), factor * values, values)


def steps_of(rng, shape, shards, low, top_value):
    factor_of = 1.0
    for axis_at, blocks in shards:
        steps = jax.random.uniform(jax.random.fold_in(jax.random.fold_in(rng, 6), axis_at), (blocks,), jnp.float32, low / len(shards), top_value / len(shards))
        factor_of = factor_of * jnp.repeat(jnp.exp(steps), shape[axis_at] // blocks).reshape((-1,) + (1,) * (len(shape) - 1 - axis_at))
    return factor_of


def centred(key, extent, scale, reach, shards=(), dtype=jnp.bfloat16):
    result = scale * jax.random.normal(key, extent, jnp.float32)
    if shards:
        result = result * steps_of(key, extent, shards, -0.22, 0.18)
    return jnp.clip(result, -reach, reach).astype(dtype)


def gaussian_with(rng, dims, spread, limit, cuts, heavy, held_as=jnp.bfloat16):
    values = spread * jax.random.normal(rng, dims, jnp.float32)
    if cuts:
        values = values * steps_of(rng, dims, cuts, -0.22, 0.18)
    return jnp.clip(with_spikes(values, jax.random.fold_in(rng, 3), *heavy), -limit, limit).astype(held_as)


def setup_inputs(seed: int = 0) -> dict:
    arg_keys = jax.random.split(jax.random.key(seed), 8)
    features = centred(arg_keys[0], (NODES, F), 1.0, 6.0, ((0, 512),))
    weight = centred(arg_keys[1], (F, F), F ** -0.5, 0.375)
    block_values = centred(arg_keys[2], (ROW_TILES, COL_TILES, BLOCKS_TILE, BLOCK, BLOCK), (BLOCK * COL_TILES) ** -0.5, 0.09375, ((0, 16), (1, 32)))
    block_rows = draw_block_rows(jax.random.fold_in(arg_keys[7], 71), 0)
    block_cols = draw_block_cols(jax.random.fold_in(arg_keys[7], 71), 0)
    counts = draw_counts(jax.random.fold_in(arg_keys[7], 71), 0)
    cotangent = gaussian_with(arg_keys[6], (NODES, F), 1.0, 24.0, ((0, 512),), (0, 1, 256, 6.0))
    return dict(features=features, weight=weight, block_values=block_values, block_rows=block_rows, block_cols=block_cols, counts=counts, cotangent=cotangent)


def gelu_tanh(value):
    return jax.nn.gelu(value, approximate=True)

def tile_forward(tiles, rows_ids, cols_ids, count, panel):
    pieces = panel[cols_ids]
    product = jnp.einsum('gab,gbf->gaf', tiles.astype(jnp.float32), pieces.astype(jnp.float32))
    alive_mask = (jnp.arange(BLOCKS_TILE) < count).astype(jnp.float32)
    product = product * alive_mask[:, None, None]
    return jnp.zeros((TILE_BR, BLOCK, F), jnp.float32).at[rows_ids].add(product)

def tile_backward(tiles, rows_ids, cols_ids, count, panel):
    pieces = panel[rows_ids]
    product = jnp.einsum('gba,gbf->gaf', tiles.astype(jnp.float32), pieces.astype(jnp.float32))
    alive_mask = (jnp.arange(BLOCKS_TILE) < count).astype(jnp.float32)
    product = product * alive_mask[:, None, None]
    return jnp.zeros((TILE_BC, BLOCK, F), jnp.float32).at[cols_ids].add(product)

def reference(features, weight, block_values, block_rows, block_cols, counts, cotangent):
    feature_blocks = features.reshape(COL_TILES, TILE_BC, BLOCK, F)

    def row_tile(row_index):

        def advance(total, col_index):
            partial_value = tile_forward(block_values[row_index, col_index], block_rows[row_index, col_index], block_cols[row_index, col_index], counts[row_index, col_index], feature_blocks[col_index])
            rounded = lax.optimization_barrier(partial_value.astype(jnp.bfloat16))
            return (total + rounded.astype(jnp.float32), None)
        total, _ = lax.scan(advance, jnp.zeros((TILE_BR, BLOCK, F), jnp.float32), jnp.arange(COL_TILES))
        return total.astype(jnp.bfloat16)
    aggregated = lax.map(row_tile, jnp.arange(ROW_TILES)).reshape(NODES, F)
    preact = jnp.dot(aggregated, weight, preferred_element_type=jnp.float32)
    activations = gelu_tanh(preact).astype(jnp.bfloat16)
    _, pullback = jax.vjp(gelu_tanh, preact)
    grad_pre = pullback(cotangent.astype(jnp.float32))[0].astype(jnp.bfloat16)
    weight_grad = lax.dot_general(aggregated, grad_pre, (((0,), (0,)), ((), ())), preferred_element_type=jnp.float32) * (1.0 / math.sqrt(NODES))
    grad_agg = lax.dot_general(grad_pre, weight, (((1,), (1,)), ((), ())), preferred_element_type=jnp.float32).astype(jnp.bfloat16)
    grad_blocks = grad_agg.reshape(ROW_TILES, TILE_BR, BLOCK, F)

    def col_tile(col_index):

        def advance(total, row_index):
            partial_value = tile_backward(block_values[row_index, col_index], block_rows[row_index, col_index], block_cols[row_index, col_index], counts[row_index, col_index], grad_blocks[row_index])
            rounded = lax.optimization_barrier(partial_value.astype(jnp.bfloat16))
            return (total + rounded.astype(jnp.float32), None)
        total, _ = lax.scan(advance, jnp.zeros((TILE_BC, BLOCK, F), jnp.float32), jnp.arange(ROW_TILES))
        return total.astype(jnp.bfloat16)
    feature_grad = lax.map(col_tile, jnp.arange(COL_TILES)).reshape(NODES, F)
    return (activations, feature_grad, weight_grad)
```

```python
import functools
import math

import jax
import jax.numpy as jnp
from jax import lax
from jax.experimental import pallas as pl
from jax.experimental.pallas import tpu as pltpu
from jax.sharding import PartitionSpec as P

bf16 = jnp.bfloat16
f32 = jnp.float32


def params(mib=48):
    return pltpu.CompilerParams(vmem_limit_bytes=mib * 1024 * 1024)


def forward_kernel(rows_ref, cols_ref, count_ref, core_ref, panel_ref, tiles_ref, keep_ref, send_ref, acc_ref):
    acc_ref[...] = jnp.zeros_like(acc_ref)
    count = count_ref[0]
    core = core_ref[0]

    def one(s):
        return jnp.dot(tiles_ref[s], panel_ref[cols_ref[s]], preferred_element_type=f32)

    def pair(t, carry):
        s = 2 * t
        first = one(s)
        second = one(s + 1)
        acc_ref[rows_ref[s]] += first
        acc_ref[rows_ref[s + 1]] += second
        return carry

    lax.fori_loop(0, count // 2, pair, 0)

    @pl.when(count % 2 == 1)
    def _():
        s = count - 1
        acc_ref[rows_ref[s]] += one(s)

    def flush(t, carry):
        keep_ref[t] = acc_ref[2 * t + core].astype(bf16)
        send_ref[t] = acc_ref[2 * t + 1 - core].astype(bf16)
        return carry

    lax.fori_loop(0, keep_ref.shape[0], flush, 0)


def forward_tiles(rows_ids, cols_ids, count, core, panel, tiles, brows):
    block, width = panel.shape[1:]
    half = jax.ShapeDtypeStruct((brows // 2, block, width), bf16)
    smem = pl.BlockSpec(memory_space=pltpu.SMEM)
    vmem = pl.BlockSpec(memory_space=pltpu.VMEM)
    return pl.pallas_call(
        forward_kernel,
        out_shape=(half, half),
        in_specs=[smem, smem, smem, smem, vmem, vmem],
        out_specs=(vmem, vmem),
        scratch_shapes=[pltpu.VMEM((brows, block, width), f32)],
        compiler_params=params(),
        name="forward_tiles",
    )(rows_ids, cols_ids, count, core, panel, tiles)


def backward_kernel(rows_ref, cols_ref, count_ref, core_ref, mine_ref, other_ref, tiles_ref, out_ref, acc_ref, grads_ref):
    acc_ref[...] = jnp.zeros_like(acc_ref)
    count = count_ref[0]
    core = core_ref[0]

    def place(t, carry):
        grads_ref[2 * t + core] = mine_ref[t]
        grads_ref[2 * t + 1 - core] = other_ref[t]
        return carry

    lax.fori_loop(0, mine_ref.shape[0], place, 0)

    def one(s):
        return lax.dot_general(
            tiles_ref[s], grads_ref[rows_ref[s]], (((0,), (0,)), ((), ())), preferred_element_type=f32
        )

    def pair(t, carry):
        s = 2 * t
        first = one(s)
        second = one(s + 1)
        acc_ref[cols_ref[s]] += first
        acc_ref[cols_ref[s + 1]] += second
        return carry

    lax.fori_loop(0, count // 2, pair, 0)

    @pl.when(count % 2 == 1)
    def _():
        s = count - 1
        acc_ref[cols_ref[s]] += one(s)

    def flush(t, carry):
        out_ref[t] = acc_ref[t].astype(bf16)
        return carry

    lax.fori_loop(0, out_ref.shape[0], flush, 0)


def backward_tiles(rows_ids, cols_ids, count, core, mine, other, tiles, bcols):
    half, block, width = mine.shape
    smem = pl.BlockSpec(memory_space=pltpu.SMEM)
    vmem = pl.BlockSpec(memory_space=pltpu.VMEM)
    return pl.pallas_call(
        backward_kernel,
        out_shape=jax.ShapeDtypeStruct((bcols, block, width), bf16),
        in_specs=[smem, smem, smem, smem, vmem, vmem, vmem],
        out_specs=vmem,
        scratch_shapes=[pltpu.VMEM((bcols, block, width), f32), pltpu.VMEM((2 * half, block, width), bf16)],
        compiler_params=params(),
        name="backward_tiles",
    )(rows_ids, cols_ids, count, core, mine, other, tiles)


def dense_kernel(parts_ref, weight_ref, cotangent_ref, act_ref, grad_agg_ref, weight_term_ref):
    total = parts_ref[0].astype(f32)
    for k in range(1, parts_ref.shape[0]):
        total += parts_ref[k].astype(f32)
    aggregated = total.astype(bf16)
    weight = weight_ref[...]
    preact = jnp.dot(aggregated, weight, preferred_element_type=f32)
    scale = math.sqrt(2 / math.pi)
    square = preact * preact
    tanh = jnp.tanh(scale * (preact + 0.044715 * (square * preact)))
    act_ref[...] = (0.5 * preact * (1.0 + tanh)).astype(bf16)
    slope = 0.5 * (1.0 + tanh) + (0.5 * preact) * (1.0 - tanh * tanh) * (
        scale * (1.0 + (3 * 0.044715) * square)
    )
    grad_pre = (cotangent_ref[...].astype(f32) * slope).astype(bf16)
    weight_term_ref[...] = lax.dot_general(
        aggregated, grad_pre, (((0,), (0,)), ((), ())), preferred_element_type=f32
    )
    grad_agg_ref[...] = lax.dot_general(
        grad_pre, weight, (((1,), (1,)), ((), ())), preferred_element_type=f32
    ).astype(bf16)


def dense(parts, weight, cotangent):
    rows, width = cotangent.shape
    vmem = pl.BlockSpec(memory_space=pltpu.VMEM)
    return pl.pallas_call(
        dense_kernel,
        out_shape=(
            jax.ShapeDtypeStruct((rows, width), bf16),
            jax.ShapeDtypeStruct((rows, width), bf16),
            jax.ShapeDtypeStruct((width, width), f32),
        ),
        in_specs=[vmem] * 3,
        out_specs=(vmem,) * 3,
        compiler_params=params(),
        name="dense",
    )(parts, weight, cotangent)


def spread(shard, axis, groups=None, count=None):
    copies = jnp.broadcast_to(shard[None], (count or lax.axis_size(axis),) + shard.shape)
    return lax.all_to_all(copies, axis, 0, 0, axis_index_groups=groups)


def local(features, weight, block_values, block_rows, block_cols, counts, cotangent):
    rows_dev, width = features.shape
    block = block_values.shape[-1]
    row_count = lax.axis_size("row")
    col_count = lax.axis_size("col")
    node_total = rows_dev * row_count * col_count
    tile_brows = rows_dev * col_count // block
    tile_bcols = rows_dev * row_count // block
    half = col_count // 2
    pairs = [(i, i ^ 1) for i in range(col_count)]
    groups = [[2 * k + c for k in range(half)] for c in range(2)]
    tiles = block_values[0, 0]
    rows_ids = block_rows[0, 0]
    cols_ids = block_cols[0, 0]
    count = counts[0]
    core = jnp.reshape(lax.axis_index("col") % 2, (1,)).astype(jnp.int32)

    panel = spread(features, "row")
    keep, send = forward_tiles(rows_ids, cols_ids, count, core, panel, tiles, tile_brows)
    came = lax.ppermute(send, "col", pairs)
    summed = (keep.astype(f32) + came.astype(f32)).astype(bf16)
    parts = lax.all_to_all(summed, "col", 0, 0, axis_index_groups=groups)
    activations, grad_agg, weight_term = dense(parts, weight, cotangent)

    mine = spread(grad_agg, "col", groups, half)
    other = lax.ppermute(mine, "col", pairs)
    weight_parts = lax.all_to_all(weight_term.reshape(col_count, width // col_count, width), "col", 0, 0)
    weight_rows = jnp.sum(weight_parts, axis=0)
    back = backward_tiles(rows_ids, cols_ids, count, core, mine, other, tiles, tile_bcols)
    weight_rows = jnp.sum(spread(weight_rows, "row"), axis=0) * (1.0 / math.sqrt(node_total))
    back_parts = lax.all_to_all(back, "row", 0, 0)
    feature_grad = jnp.sum(back_parts.astype(f32), axis=0).astype(bf16)
    weight_grad = spread(weight_rows, "col").reshape(width, width)
    return (activations, feature_grad, weight_grad)


def solution(mesh):
    in_specs = (
        P(("col", "row"), None),
        P(),
        P("row", "col", None, None, None),
        P("row", "col", None),
        P("row", "col", None),
        P("row", "col"),
        P(("row", "col"), None),
    )
    out_specs = (P(("row", "col"), None), P(("col", "row"), None), P())
    return jax.shard_map(local, mesh=mesh, in_specs=in_specs, out_specs=out_specs, check_vma=False)
```

```python
import math

import jax
import jax.numpy as jnp
from jax import lax
from jax.experimental import pallas as pl
from jax.experimental.pallas import tpu as pltpu
from jax.sharding import PartitionSpec as P

bf16 = jnp.bfloat16
f32 = jnp.float32
i32 = jnp.int32
smem = pl.BlockSpec(memory_space=pltpu.SMEM)
vmem = pl.BlockSpec(memory_space=pltpu.VMEM)
row_base = 4
col_base = 8
quad = 4


def params(mib=48):
    return pltpu.CompilerParams(vmem_limit_bytes=mib * 1024 * 1024)


def cost(flops, moved):
    return pl.CostEstimate(flops=flops, bytes_accessed=moved, transcendentals=0)


def sort_slots(ids_ref, count, base_ref, extra_ref, extra_ids_ref, total_ref, seen_ref, last_ref, base):
    zero_slot = ids_ref.shape[0]
    targets = base_ref.shape[0] // base

    def clear_base(t, carry):
        base_ref[t] = zero_slot
        return carry

    def clear_extra(t, carry):
        extra_ref[t] = zero_slot
        return carry

    def clear_seen(t, carry):
        seen_ref[t] = 0
        return carry

    lax.fori_loop(0, base_ref.shape[0], clear_base, 0)
    lax.fori_loop(0, extra_ref.shape[0], clear_extra, 0)
    lax.fori_loop(0, targets, clear_seen, 0)
    total_ref[0] = 0

    def place(s, carry):
        target = ids_ref[s]
        seen = seen_ref[target]
        seen_ref[target] = seen + 1

        @pl.when(seen < base)
        def _():
            base_ref[target * base + seen] = s

        @pl.when(seen >= base)
        def _():
            over = (seen - base) % quad

            @pl.when(over == 0)
            def _():
                group = total_ref[0]
                total_ref[0] = group + 1
                last_ref[target] = group
                extra_ids_ref[group] = target

            extra_ref[last_ref[target] * quad + over] = s

        return carry

    lax.fori_loop(0, count, place, 0)


def prepare_kernel(
    rows_ref, cols_ref, count_ref, tiles_ref,
    by_row_ref, more_by_row_ref, more_rows_ref, row_total_ref,
    by_col_ref, more_by_col_ref, more_cols_ref, col_total_ref,
    rows_out_ref, cols_out_ref, plain_ref, flipped_ref,
    seen_ref, last_ref,
):
    slots = tiles_ref.shape[0]
    count = count_ref[0]
    sort_slots(rows_ref, count, by_row_ref, more_by_row_ref, more_rows_ref, row_total_ref, seen_ref, last_ref, row_base)
    sort_slots(cols_ref, count, by_col_ref, more_by_col_ref, more_cols_ref, col_total_ref, seen_ref, last_ref, col_base)

    def copy_ids(s, carry):
        rows_out_ref[s] = rows_ref[s]
        cols_out_ref[s] = cols_ref[s]
        return carry

    lax.fori_loop(0, slots, copy_ids, 0)
    rows_out_ref[slots] = 0
    cols_out_ref[slots] = 0

    def copy_tile(s, carry):
        tile = tiles_ref[s]
        plain_ref[s] = tile
        flipped_ref[s] = tile.T
        return carry

    lax.fori_loop(0, slots, copy_tile, 0)
    plain_ref[slots] = jnp.zeros(plain_ref.shape[1:], bf16)
    flipped_ref[slots] = jnp.zeros(plain_ref.shape[1:], bf16)


def prepare(rows_ids, cols_ids, count, tiles, brows, bcols):
    slots, block, _ = tiles.shape
    ints = lambda size: jax.ShapeDtypeStruct((size,), i32)
    held = jax.ShapeDtypeStruct((slots + 1, block, block), bf16)
    lists = lambda targets, base: (ints(targets * base), ints(slots * quad), ints(slots), ints(1))
    return pl.pallas_call(
        prepare_kernel,
        out_shape=(*lists(brows, row_base), *lists(bcols, col_base), ints(slots + 1), ints(slots + 1), held, held),
        in_specs=[smem, smem, smem, vmem],
        out_specs=(smem,) * 10 + (vmem, vmem),
        scratch_shapes=[pltpu.SMEM((max(brows, bcols),), i32), pltpu.SMEM((max(brows, bcols),), i32)],
        compiler_params=params(),
        cost_estimate=cost(0, 9 * slots * block * block * 2),
        name="prepare",
    )(rows_ids, cols_ids, count, tiles)


def grouped_product(tiles_ref, ids_ref, source, list_ref, first, size):
    slots = [list_ref[first + k] for k in range(size)]
    left = jnp.concatenate([tiles_ref[s] for s in slots], axis=1)
    right = jnp.concatenate([source(ids_ref[s]) for s in slots], axis=0)
    return jnp.dot(left, right, preferred_element_type=f32)


def forward_kernel(
    by_row_ref, more_ref, more_rows_ref, total_ref, cols_ref, core_ref, panel_ref, tiles_ref, keep_ref, send_ref, acc_ref
):
    core = core_ref[0]
    source = lambda c: panel_ref[c]

    def base(t, carry):
        acc_ref[t] = grouped_product(tiles_ref, cols_ref, source, by_row_ref, t * row_base, row_base)
        return carry

    lax.fori_loop(0, acc_ref.shape[0], base, 0, unroll=4)

    def more(t, carry):
        acc_ref[more_rows_ref[t]] += grouped_product(tiles_ref, cols_ref, source, more_ref, t * quad, quad)
        return carry

    lax.fori_loop(0, total_ref[0], more, 0)

    def flush(t, carry):
        keep_ref[t] = acc_ref[2 * t + core].astype(bf16)
        send_ref[t] = acc_ref[2 * t + 1 - core].astype(bf16)
        return carry

    lax.fori_loop(0, keep_ref.shape[0], flush, 0)


def forward_tiles(by_row, more, more_rows, total, cols_ids, core, panel, tiles, brows):
    block, width = panel.shape[1:]
    half = jax.ShapeDtypeStruct((brows // 2, block, width), bf16)
    return pl.pallas_call(
        forward_kernel,
        out_shape=(half, half),
        in_specs=[smem] * 6 + [vmem, vmem],
        out_specs=(vmem, vmem),
        scratch_shapes=[pltpu.VMEM((brows, block, width), f32)],
        compiler_params=params(),
        cost_estimate=cost(2 * brows * row_base * block * block * width, tiles.size * 2),
        name="forward_tiles",
    )(by_row, more, more_rows, total, cols_ids, core, panel, tiles)


def sum_parts(ref):
    total = ref[0].astype(f32)
    for k in range(1, ref.shape[0]):
        total += ref[k].astype(f32)
    return total


def dense_kernel(parts_ref, weight_ref, cotangent_ref, act_ref, message_ref):
    aggregated = sum_parts(parts_ref)
    aggregated_half = aggregated.astype(bf16)
    preact = jnp.dot(aggregated_half, weight_ref[...], preferred_element_type=f32)
    scale = math.sqrt(2 / math.pi)
    square = preact * preact
    tanh = jnp.tanh(scale * (preact + 0.044715 * (square * preact)))
    act_ref[...] = (0.5 * preact * (1.0 + tanh)).astype(bf16)
    slope = 0.5 * (1.0 + tanh) + (0.5 * preact) * (1.0 - tanh * tanh) * (
        scale * (1.0 + (3 * 0.044715) * square)
    )
    grad_pre = (cotangent_ref[...].astype(f32) * slope).astype(bf16)
    turned = aggregated_half.astype(f32).T
    peers = message_ref.shape[0]
    rows = grad_pre.shape[0]
    own = turned.shape[0] // peers
    for k in range(peers):
        message_ref[k, :rows, :] = grad_pre
        low = turned[k * own : k * own + own // 2]
        high = turned[k * own + own // 2 : (k + 1) * own]
        message_ref[k, rows:, :] = jnp.concatenate([low, high], axis=1).astype(bf16)


def dense(parts, weight, cotangent):
    rows, width = cotangent.shape
    peers = parts.shape[0]
    return pl.pallas_call(
        dense_kernel,
        out_shape=(
            jax.ShapeDtypeStruct((rows, width), bf16),
            jax.ShapeDtypeStruct((peers, rows + rows // peers, width), bf16),
        ),
        in_specs=[vmem] * 3,
        out_specs=(vmem,) * 2,
        compiler_params=params(),
        name="dense",
    )(parts, weight, cotangent)


def weight_kernel(message_ref, out_ref):
    peers, _, width = message_ref.shape
    rows = width // 2
    total = None
    for k in range(peers):
        packed = message_ref[k, rows:, :].astype(f32)
        left = jnp.concatenate([packed[:, :rows], packed[:, rows:]], axis=0).astype(bf16)
        term = jnp.dot(left, message_ref[k, :rows, :], preferred_element_type=f32)
        total = term if total is None else total + term
    for k in range(out_ref.shape[0]):
        out_ref[k] = total


def weight_part(message, copies):
    peers, _, width = message.shape
    return pl.pallas_call(
        weight_kernel,
        out_shape=jax.ShapeDtypeStruct((copies, width // peers, width), f32),
        in_specs=[vmem],
        out_specs=vmem,
        compiler_params=params(),
        name="weight_part",
    )(message)


def backward_kernel(by_col_ref, more_ref, more_cols_ref, total_ref, rows_ref, core_ref, mine_ref, other_ref, tiles_ref, out_ref, acc_ref, grads_ref):
    core = core_ref[0]
    block = out_ref.shape[1]

    def place(t, carry):
        grads_ref[2 * t + core] = mine_ref[t, :block, :]
        grads_ref[2 * t + 1 - core] = other_ref[t, :block, :]
        return carry

    lax.fori_loop(0, mine_ref.shape[0], place, 0)
    source = lambda r: grads_ref[r]

    def base(t, carry):
        acc_ref[t] = grouped_product(tiles_ref, rows_ref, source, by_col_ref, t * col_base, col_base)
        return carry

    lax.fori_loop(0, acc_ref.shape[0], base, 0, unroll=2)

    def more(t, carry):
        acc_ref[more_cols_ref[t]] += grouped_product(tiles_ref, rows_ref, source, more_ref, t * quad, quad)
        return carry

    lax.fori_loop(0, total_ref[0], more, 0)

    def flush(t, carry):
        out_ref[t] = acc_ref[t].astype(bf16)
        return carry

    lax.fori_loop(0, out_ref.shape[0], flush, 0)


def backward_tiles(by_col, more, more_cols, total, rows_ids, core, mine, other, tiles, bcols):
    half, _, width = mine.shape
    block = tiles.shape[-1]
    return pl.pallas_call(
        backward_kernel,
        out_shape=jax.ShapeDtypeStruct((bcols, block, width), bf16),
        in_specs=[smem] * 6 + [vmem] * 3,
        out_specs=vmem,
        scratch_shapes=[pltpu.VMEM((bcols, block, width), f32), pltpu.VMEM((2 * half, block, width), bf16)],
        compiler_params=params(),
        cost_estimate=cost(2 * bcols * col_base * block * block * width, tiles.size * 2),
        name="backward_tiles",
    )(by_col, more, more_cols, total, rows_ids, core, mine, other, tiles)


def finish_kernel(parts_ref, weight_ref, out_ref):
    total = sum_parts(parts_ref).astype(bf16)
    out_ref[...] = lax.dot_general(
        total, weight_ref[...], (((1,), (1,)), ((), ())), preferred_element_type=f32
    ).astype(bf16)


def finish(parts, weight):
    return pl.pallas_call(
        finish_kernel,
        out_shape=jax.ShapeDtypeStruct(parts.shape[1:], bf16),
        in_specs=[vmem] * 2,
        out_specs=vmem,
        compiler_params=params(),
        name="finish",
    )(parts, weight)


def gather_over_col(rows, me, size):
    held = rows + lax.ppermute(rows, "col", [(i, i ^ 1) for i in range(size)])
    held = held[None]
    distance = 2
    while distance < size:
        came = lax.ppermute(held, "col", [(i, i ^ distance) for i in range(size)])
        upper = (me // distance) % 2 == 1
        held = jnp.where(upper, jnp.concatenate([came, held]), jnp.concatenate([held, came]))
        distance *= 2
    return held.reshape(-1, rows.shape[-1])


def local(features, weight, block_values, block_rows, block_cols, counts, cotangent):
    rows_dev, width = features.shape
    block = block_values.shape[-1]
    row_count = lax.axis_size("row")
    col_count = lax.axis_size("col")
    node_total = rows_dev * row_count * col_count
    brows = rows_dev * col_count // block
    bcols = rows_dev * row_count // block
    half = col_count // 2
    pairs = [(i, i ^ 1) for i in range(col_count)]
    groups = [[2 * k + c for k in range(half)] for c in range(2)]
    me = lax.axis_index("col")
    core = jnp.reshape(me % 2, (1,)).astype(i32)

    copies = jnp.broadcast_to(features[None], (row_count,) + features.shape)
    panel = lax.all_to_all(copies, "row", 0, 0)
    lists = prepare(block_rows[0, 0], block_cols[0, 0], counts[0], block_values[0, 0], brows, bcols)
    row_lists, col_lists = lists[:4], lists[4:8]
    rows_ids, cols_ids, tiles, flipped = lists[8:]

    keep, send = forward_tiles(*row_lists, cols_ids, core, panel, tiles, brows)
    came = lax.ppermute(send, "col", pairs)
    summed = (keep.astype(f32) + came.astype(f32)).astype(bf16)
    parts = lax.all_to_all(summed, "col", 0, 0, axis_index_groups=groups)
    activations, messages = dense(parts, weight, cotangent)

    mine = lax.all_to_all(messages, "col", 0, 0, axis_index_groups=groups)
    other = lax.ppermute(mine, "col", pairs)
    weight_parts = lax.all_to_all(weight_part(mine, row_count), "row", 0, 0)
    back = backward_tiles(*col_lists, rows_ids, core, mine, other, flipped, bcols)
    back_parts = lax.all_to_all(back, "row", 0, 0)
    weight_rows = jnp.sum(weight_parts, axis=0) * (1.0 / math.sqrt(node_total))
    weight_grad = gather_over_col(weight_rows, me, col_count)
    feature_grad = finish(back_parts, weight)
    return (activations, feature_grad, weight_grad)


def solution(mesh):
    in_specs = (
        P(("col", "row"), None),
        P(),
        P("row", "col", None, None, None),
        P("row", "col", None),
        P("row", "col", None),
        P("row", "col"),
        P(("row", "col"), None),
    )
    out_specs = (P(("row", "col"), None), P(("col", "row"), None), P())
    return jax.shard_map(local, mesh=mesh, in_specs=in_specs, out_specs=out_specs, check_vma=False)
```

```python
import functools
import math

import jax
import jax.numpy as jnp
from jax import lax
from jax.experimental import pallas as pl
from jax.experimental.pallas import tpu as pltpu
from jax.sharding import PartitionSpec as P

bf16 = jnp.bfloat16
f32 = jnp.float32
i32 = jnp.int32
smem = pl.BlockSpec(memory_space=pltpu.SMEM)
vmem = pl.BlockSpec(memory_space=pltpu.VMEM)
quad = 4


def params(mib=16):
    return pltpu.CompilerParams(vmem_limit_bytes=mib * 1024 * 1024)


def cost(flops, moved):
    return pl.CostEstimate(flops=flops, bytes_accessed=moved, transcendentals=0)


def sort_slots(target_of, slots, count, base_ref, extra_ref, extra_ids_ref, total_ref, seen_ref, last_ref):
    zero_slot = slots
    size = quad
    targets = base_ref.shape[0] // size

    def clear_base(t, carry):
        base_ref[t] = zero_slot
        return carry

    def clear_extra(t, carry):
        extra_ref[t] = zero_slot
        return carry

    def clear_seen(t, carry):
        seen_ref[t] = 0
        return carry

    lax.fori_loop(0, base_ref.shape[0], clear_base, 0)
    lax.fori_loop(0, extra_ref.shape[0], clear_extra, 0)
    lax.fori_loop(0, targets, clear_seen, 0)
    total_ref[0] = 0

    def place(s, carry):
        target = target_of(s)
        seen = seen_ref[target]
        seen_ref[target] = seen + 1

        @pl.when(seen < size)
        def _():
            base_ref[target * size + seen] = s

        @pl.when(seen >= size)
        def _():
            over = seen % size

            @pl.when(over == 0)
            def _():
                group = total_ref[0]
                total_ref[0] = group + 1
                last_ref[target] = group
                extra_ids_ref[group] = 2 * target + (seen == size).astype(i32)

            extra_ref[last_ref[target] * size + over] = s

        return carry

    lax.fori_loop(0, count, place, 0)


def prepare_kernel(
    rows_ref, cols_ref, count_ref, core_ref, tiles_ref,
    fwd_ref, fwd_more_ref, fwd_more_ids_ref, fwd_total_ref, fwd_source_ref,
    bwd_ref, bwd_more_ref, bwd_more_ids_ref, bwd_total_ref, bwd_source_ref,
    flipped_ref, seen_ref, last_ref,
):
    slots = rows_ref.shape[0]
    count = count_ref[0]
    core = core_ref[0]
    half = fwd_ref.shape[0] // (2 * quad)

    def away(s):
        return (rows_ref[s] % 2 != core).astype(i32)

    def forward_target(s):
        return away(s) * half + rows_ref[s] // 2

    def backward_target(s):
        return away(s) * half + cols_ref[s]

    sort_slots(forward_target, slots, count, fwd_ref, fwd_more_ref, fwd_more_ids_ref, fwd_total_ref, seen_ref, last_ref)
    sort_slots(backward_target, slots, count, bwd_ref, bwd_more_ref, bwd_more_ids_ref, bwd_total_ref, seen_ref, last_ref)

    def sources(s, carry):
        fwd_source_ref[s] = cols_ref[s]
        bwd_source_ref[s] = rows_ref[s] // 2
        return carry

    lax.fori_loop(0, slots, sources, 0)
    fwd_source_ref[slots] = 0
    bwd_source_ref[slots] = 0

    def turn(s, carry):
        flipped_ref[s] = tiles_ref[s].T
        return carry

    lax.fori_loop(0, slots, turn, 0, unroll=4)
    flipped_ref[slots] = jnp.zeros(flipped_ref.shape[1:], bf16)


def prepare(rows_ids, cols_ids, count, core, tiles, targets):
    slots, block, _ = tiles.shape
    ints = lambda size: jax.ShapeDtypeStruct((size,), i32)
    held = jax.ShapeDtypeStruct((slots + 1, block, block), bf16)
    lists = (ints(targets * quad), ints(slots * quad), ints(slots), ints(1), ints(slots + 1))
    return pl.pallas_call(
        prepare_kernel,
        out_shape=(*lists, *lists, held),
        in_specs=[smem] * 4 + [vmem],
        out_specs=(smem,) * 10 + (vmem,),
        scratch_shapes=[pltpu.SMEM((targets,), i32)] * 2,
        compiler_params=params(24),
        cost_estimate=cost(0, 9 * slots * block * block * 2),
        name="prepare",
    )(rows_ids, cols_ids, count, core, tiles)


def grouped_product(tiles_ref, ids_ref, source_ref, list_ref, group):
    slots = [list_ref[group * quad + k] for k in range(quad)]
    block = tiles_ref.shape[1]
    held = tiles_ref.shape[0]
    if held == ids_ref.shape[0]:
        parts = [tiles_ref[s] for s in slots]
    else:
        parts = [tiles_ref[jnp.minimum(s, held - 1)] for s in slots]
        parts = [jnp.where(s < held, part, jnp.zeros_like(part)) for s, part in zip(slots, parts)]
    left = jnp.concatenate(parts, axis=1)
    right = jnp.concatenate([source_ref[ids_ref[s], :block, :] for s in slots], axis=0)
    return jnp.dot(left, right, preferred_element_type=f32)


def further_groups(lists, tiles_ref, source_ref, acc_ref, first, targets, store):
    list_ref, more_ref, more_ids_ref, total_ref, ids_ref = lists

    def more(t, carry):
        code = more_ids_ref[t]
        target = code // 2
        place = target - first

        @pl.when((place >= 0) & (place < targets))
        def _():
            @pl.when(code % 2 == 1)
            def _():
                acc_ref[place] = grouped_product(tiles_ref, ids_ref, source_ref, list_ref, target)

            acc_ref[place] += grouped_product(tiles_ref, ids_ref, source_ref, more_ref, t)
            store(place)

        return carry

    lax.fori_loop(0, total_ref[0], more, 0)


def forward_kernel(part, *refs):
    lists = refs[:5]
    panel_ref, tiles_ref, out_ref, acc_ref = refs[5:]
    half = out_ref.shape[0]

    def base(t, carry):
        product = grouped_product(tiles_ref, lists[4], panel_ref, lists[0], part * half + t)
        out_ref[t] = product.astype(bf16)
        return carry

    lax.fori_loop(0, half, base, 0, unroll=4)

    def store(place):
        out_ref[place] = acc_ref[place].astype(bf16)

    further_groups(lists, tiles_ref, panel_ref, acc_ref, part * half, half, store)


def forward_tiles(part, lists, panel, tiles):
    block, width = panel.shape[1:]
    shape = (lists[0].shape[0] // (2 * quad), block, width)
    return pl.pallas_call(
        functools.partial(forward_kernel, part),
        out_shape=jax.ShapeDtypeStruct(shape, bf16),
        in_specs=[smem] * 5 + [vmem] * 2,
        out_specs=vmem,
        scratch_shapes=[pltpu.VMEM(shape, f32)],
        compiler_params=params(),
        cost_estimate=cost(2 * shape[0] * quad * block * block * width, tiles.size),
        name="forward_tiles_%d" % part,
    )(*lists, panel, tiles)


def spread_kernel(in_ref, out_ref):
    for k in range(out_ref.shape[0]):
        out_ref[k] = in_ref[...]


def spread(shard, copies):
    return pl.pallas_call(
        spread_kernel,
        out_shape=pltpu.VMEM((copies,) + shard.shape, shard.dtype),
        in_specs=[vmem],
        out_specs=vmem,
        compiler_params=params(),
        name="spread",
    )(shard)


def sum_parts(ref):
    total = ref[0].astype(f32)
    for k in range(1, ref.shape[0]):
        total += ref[k].astype(f32)
    return total


def dense_kernel(parts_ref, weight_ref, cotangent_ref, act_ref, message_ref):
    aggregated = sum_parts(parts_ref)
    aggregated_half = aggregated.astype(bf16)
    preact = jnp.dot(aggregated_half, weight_ref[...], preferred_element_type=f32)
    scale = math.sqrt(2 / math.pi)
    square = preact * preact
    tanh = jnp.tanh(scale * (preact + 0.044715 * (square * preact)))
    act_ref[...] = (0.5 * preact * (1.0 + tanh)).astype(bf16)
    slope = 0.5 * (1.0 + tanh) + (0.5 * preact) * (1.0 - tanh * tanh) * (
        scale * (1.0 + (3 * 0.044715) * square)
    )
    grad_pre = (cotangent_ref[...].astype(f32) * slope).astype(bf16)
    turned = aggregated_half.astype(f32).T
    peers = message_ref.shape[0]
    rows = grad_pre.shape[0]
    own = 2 * turned.shape[0] // peers
    for k in range(peers):
        message_ref[k, :rows, :] = grad_pre
        first = (k // 2) * own
        low = turned[first : first + own // 2]
        high = turned[first + own // 2 : first + own]
        message_ref[k, rows:, :] = jnp.concatenate([low, high], axis=1).astype(bf16)


def dense(parts, weight, cotangent):
    rows, width = cotangent.shape
    peers = parts.shape[0]
    return pl.pallas_call(
        dense_kernel,
        out_shape=(
            jax.ShapeDtypeStruct((rows, width), bf16),
            jax.ShapeDtypeStruct((peers, rows + width // peers, width), bf16),
        ),
        in_specs=[vmem] * 3,
        out_specs=(vmem,) * 2,
        compiler_params=params(),
        name="dense",
    )(parts, weight, cotangent)


def weight_kernel(mine_ref, out_ref):
    peers, _, width = mine_ref.shape
    rows = width // 2
    total = None
    for k in range(0, peers, 2):
        left = []
        for p in (k, k + 1):
            packed = mine_ref[p, rows:, :].astype(f32)
            left.append(jnp.concatenate([packed[:, :rows], packed[:, rows:]], axis=0))
        left = jnp.concatenate(left, axis=1).astype(bf16)
        right = jnp.concatenate([mine_ref[k, :rows, :], mine_ref[k + 1, :rows, :]], axis=0)
        term = jnp.dot(left, right, preferred_element_type=f32)
        total = term if total is None else total + term
    rounded = total.astype(bf16)
    for k in range(out_ref.shape[0]):
        out_ref[k] = rounded


def weight_part(mine, copies):
    peers, _, width = mine.shape
    return pl.pallas_call(
        weight_kernel,
        out_shape=jax.ShapeDtypeStruct((copies, 2 * width // peers, width), bf16),
        in_specs=[vmem],
        out_specs=vmem,
        compiler_params=params(),
        cost_estimate=cost(0, mine.size),
        name="weight_part",
    )(mine)


def weight_sum_kernel(scale, parts_ref, out_ref):
    out_ref[...] = sum_parts(parts_ref) * scale


def weight_sum(parts, scale):
    return pl.pallas_call(
        functools.partial(weight_sum_kernel, scale),
        out_shape=jax.ShapeDtypeStruct(parts.shape[1:], f32),
        in_specs=[vmem],
        out_specs=vmem,
        compiler_params=params(),
        cost_estimate=cost(0, parts.size),
        name="weight_sum",
    )(parts)


def gather_over_col(rows, position, size):
    held = (rows + lax.ppermute(rows, "col", [(i, i ^ 1) for i in range(size)]))[None]
    steps = (size // 2, size // 4, size // 8)
    for distance in steps:
        came = lax.ppermute(held, "col", [(i, i ^ distance) for i in range(size)])
        if distance == steps[-1]:
            return held, came
        upper = (position // distance) % 2 == 1
        held = jnp.where(upper, jnp.concatenate([came, held]), jnp.concatenate([held, came]))


def backward_kernel(*refs):
    *refs, held_ref, held_sem = refs
    tiles_copy = pltpu.make_async_copy(refs[7], held_ref, held_sem)
    tiles_copy.start()
    tiles_copy.wait()
    lists = refs[:5]
    list_ref, more_ref, more_ids_ref, total_ref, ids_ref = lists
    mine_ref, other_ref, _, out_ref, acc_ref = refs[5:]
    tiles_ref = held_ref
    targets = out_ref.shape[0]

    def base(t, carry):
        product = grouped_product(tiles_ref, ids_ref, mine_ref, list_ref, t)
        product += grouped_product(tiles_ref, ids_ref, other_ref, list_ref, targets + t)
        acc_ref[t] = product
        out_ref[t] = product.astype(bf16)
        return carry

    lax.fori_loop(0, targets, base, 0, unroll=4)

    def more(t, carry):
        target = more_ids_ref[t] // 2
        place = target % targets

        @pl.when(target < targets)
        def _():
            acc_ref[place] += grouped_product(tiles_ref, ids_ref, mine_ref, more_ref, t)

        @pl.when(target >= targets)
        def _():
            acc_ref[place] += grouped_product(tiles_ref, ids_ref, other_ref, more_ref, t)

        out_ref[place] = acc_ref[place].astype(bf16)
        return carry

    lax.fori_loop(0, total_ref[0], more, 0)


def backward_tiles(lists, mine, other, tiles):
    width = mine.shape[-1]
    block = tiles.shape[-1]
    shape = (lists[0].shape[0] // (2 * quad), block, width)
    return pl.pallas_call(
        backward_kernel,
        out_shape=jax.ShapeDtypeStruct(shape, bf16),
        in_specs=[smem] * 5 + [vmem] * 2 + [pl.BlockSpec(memory_space=pltpu.HBM)],
        out_specs=vmem,
        scratch_shapes=[pltpu.VMEM(shape, f32), pltpu.VMEM(tiles.shape, bf16), pltpu.SemaphoreType.DMA],
        compiler_params=params(),
        cost_estimate=cost(4 * shape[0] * quad * block * block * width, tiles.size),
        name="backward_tiles",
    )(*lists, mine, other, pltpu.with_memory_space_constraint(tiles, pltpu.HBM))


def finish_kernel(upper_ref, parts_ref, weight_ref, held_ref, came_ref, out_ref, weight_out_ref):
    out_ref[...] = lax.dot_general(
        sum_parts(parts_ref).astype(bf16), weight_ref[...], (((1,), (1,)), ((), ())), preferred_element_type=f32
    ).astype(bf16)
    upper = upper_ref[0] == 1
    chunks, own, _ = held_ref.shape
    for k in range(2 * chunks):
        bits = [(k >> b) & 1 for b in range(3)]
        place = bits[1] * 2 + bits[2]
        held, came = held_ref[place], came_ref[place]
        low, high = (held, came) if bits[0] == 0 else (came, held)
        weight_out_ref[k * own : (k + 1) * own, :] = jnp.where(upper, high, low)


def finish(upper, parts, weight, held, came):
    return pl.pallas_call(
        finish_kernel,
        out_shape=(jax.ShapeDtypeStruct(parts.shape[1:], bf16), jax.ShapeDtypeStruct(weight.shape, f32)),
        in_specs=[smem] + [vmem] * 4,
        out_specs=(vmem,) * 2,
        compiler_params=params(),
        name="finish",
    )(upper, parts, weight, held, came)


def local(features, weight, block_values, block_rows, block_cols, counts, cotangent):
    rows_dev, width = features.shape
    row_count = lax.axis_size("row")
    col_count = lax.axis_size("col")
    node_total = rows_dev * row_count * col_count
    half = col_count // 2
    pairs = [(i, i ^ 1) for i in range(col_count)]
    groups = [[2 * k + c for k in range(half)] for c in range(2)]
    position = lax.axis_index("col").astype(i32)
    core = jnp.reshape(position % 2, (1,))
    tiles = block_values[0, 0]

    panel = lax.all_to_all(spread(features, row_count), "row", 0, 0)
    made = prepare(block_rows[0, 0], block_cols[0, 0], counts[0], core, tiles, col_count)
    forward_lists, (*backward_lists, backward_ids), flipped = made[:5], made[5:10], made[10]

    send = forward_tiles(1, forward_lists, panel, tiles)
    came = lax.ppermute(send, "col", pairs)
    keep = forward_tiles(0, forward_lists, panel, tiles)
    summed = (keep.astype(f32) + came.astype(f32)).astype(bf16)
    parts = lax.all_to_all(summed, "col", 0, 0, axis_index_groups=groups)
    activations, messages = dense(parts, weight, cotangent)

    mine = lax.all_to_all(messages, "col", 0, 0, axis_index_groups=groups)
    other = lax.ppermute(mine, "col", pairs)
    weight_rows, backward_ids = lax.optimization_barrier((weight_part(mine, row_count), backward_ids))
    weight_parts = lax.all_to_all(weight_rows, "row", 0, 0)
    back = backward_tiles((*backward_lists, backward_ids), mine, other, flipped)
    back_parts = lax.all_to_all(back, "row", 0, 0)
    weight_rows = weight_sum(weight_parts, 1.0 / math.sqrt(node_total))
    held, came = gather_over_col(weight_rows, position, col_count)
    upper = jnp.reshape((position // (col_count // 8)) % 2, (1,))
    feature_grad, weight_grad = finish(upper, back_parts, weight, held, came)
    return (activations, feature_grad, weight_grad)


def solution(mesh):
    in_specs = (
        P(("col", "row"), None),
        P(),
        P("row", "col", None, None, None),
        P("row", "col", None),
        P("row", "col", None),
        P("row", "col"),
        P(("row", "col"), None),
    )
    out_specs = (P(("row", "col"), None), P(("col", "row"), None), P())
    return jax.shard_map(local, mesh=mesh, in_specs=in_specs, out_specs=out_specs, check_vma=False)
```

```python
import functools
import math

import jax
import jax.numpy as jnp
from jax import lax
from jax.experimental import pallas as pl
from jax.experimental.pallas import tpu as pltpu
from jax.sharding import PartitionSpec as P

bf16 = jnp.bfloat16
f32 = jnp.float32
i32 = jnp.int32
smem = pl.BlockSpec(memory_space=pltpu.SMEM)
vmem = pl.BlockSpec(memory_space=pltpu.VMEM)
quad = 4


def params(mib=16):
    return pltpu.CompilerParams(vmem_limit_bytes=mib * 1024 * 1024)


def cost(flops, moved):
    return pl.CostEstimate(flops=flops, bytes_accessed=moved, transcendentals=0)


def sort_slots(target_of, slots, count, base_ref, extra_ref, extra_ids_ref, total_ref, seen_ref, last_ref):
    zero_slot = slots
    size = quad
    targets = base_ref.shape[0] // size

    def clear_base(t, carry):
        base_ref[t] = zero_slot
        return carry

    def clear_extra(t, carry):
        extra_ref[t] = zero_slot
        return carry

    def clear_seen(t, carry):
        seen_ref[t] = 0
        return carry

    lax.fori_loop(0, base_ref.shape[0], clear_base, 0)
    lax.fori_loop(0, extra_ref.shape[0], clear_extra, 0)
    lax.fori_loop(0, targets, clear_seen, 0)
    total_ref[0] = 0

    def place(s, carry):
        target = target_of(s)
        seen = seen_ref[target]
        seen_ref[target] = seen + 1

        @pl.when(seen < size)
        def _():
            base_ref[target * size + seen] = s

        @pl.when(seen >= size)
        def _():
            over = seen % size

            @pl.when(over == 0)
            def _():
                group = total_ref[0]
                total_ref[0] = group + 1
                last_ref[target] = group
                extra_ids_ref[group] = target

            extra_ref[last_ref[target] * size + over] = s

        return carry

    lax.fori_loop(0, count, place, 0)


def prepare_kernel(
    rows_ref, cols_ref, count_ref, core_ref, tiles_ref,
    fwd_ref, fwd_more_ref, fwd_more_ids_ref, fwd_total_ref, fwd_source_ref,
    bwd_ref, bwd_more_ref, bwd_more_ids_ref, bwd_total_ref, bwd_source_ref,
    flipped_ref, seen_ref, last_ref,
):
    slots = rows_ref.shape[0]
    count = count_ref[0]
    core = core_ref[0]
    half = fwd_ref.shape[0] // (2 * quad)

    def away(s):
        return (rows_ref[s] % 2 != core).astype(i32)

    def forward_target(s):
        return away(s) * half + rows_ref[s] // 2

    def backward_target(s):
        return away(s) * half + cols_ref[s]

    sort_slots(forward_target, slots, count, fwd_ref, fwd_more_ref, fwd_more_ids_ref, fwd_total_ref, seen_ref, last_ref)
    sort_slots(backward_target, slots, count, bwd_ref, bwd_more_ref, bwd_more_ids_ref, bwd_total_ref, seen_ref, last_ref)

    def sources(s, carry):
        fwd_source_ref[s] = cols_ref[s]
        bwd_source_ref[s] = rows_ref[s] // 2
        return carry

    lax.fori_loop(0, slots, sources, 0)
    fwd_source_ref[slots] = 0
    bwd_source_ref[slots] = 0

    def turn(s, carry):
        flipped_ref[s] = tiles_ref[s].T
        return carry

    lax.fori_loop(0, slots, turn, 0, unroll=4)
    flipped_ref[slots] = jnp.zeros(flipped_ref.shape[1:], bf16)


def prepare(rows_ids, cols_ids, count, core, tiles, targets):
    slots, block, _ = tiles.shape
    ints = lambda size: jax.ShapeDtypeStruct((size,), i32)
    held = jax.ShapeDtypeStruct((slots + 1, block, block), bf16)
    lists = (ints(targets * quad), ints(slots * quad), ints(slots), ints(1), ints(slots + 1))
    return pl.pallas_call(
        prepare_kernel,
        out_shape=(*lists, *lists, held),
        in_specs=[smem] * 4 + [vmem],
        out_specs=(smem,) * 10 + (vmem,),
        scratch_shapes=[pltpu.SMEM((targets,), i32)] * 2,
        compiler_params=params(24),
        cost_estimate=cost(0, 9 * slots * block * block * 2),
        name="prepare",
    )(rows_ids, cols_ids, count, core, tiles)


def grouped_product(tiles_ref, ids_ref, source_ref, list_ref, group):
    slots = [list_ref[group * quad + k] for k in range(quad)]
    block = tiles_ref.shape[1]
    held = tiles_ref.shape[0]
    if held == ids_ref.shape[0]:
        parts = [tiles_ref[s] for s in slots]
    else:
        parts = [tiles_ref[jnp.minimum(s, held - 1)] for s in slots]
        parts = [jnp.where(s < held, part, jnp.zeros_like(part)) for s, part in zip(slots, parts)]
    left = jnp.concatenate(parts, axis=1)
    right = jnp.concatenate([source_ref[ids_ref[s], :block, :] for s in slots], axis=0)
    return jnp.dot(left, right, preferred_element_type=f32)


def forward_kernel(part, *refs):
    lists = refs[:5]
    list_ref, more_ref, more_ids_ref, total_ref, ids_ref = lists
    panel_ref, tiles_ref, out_ref, acc_ref = refs[5:]
    half = out_ref.shape[0]

    def base(t, carry):
        product = grouped_product(tiles_ref, ids_ref, panel_ref, list_ref, part * half + t)
        acc_ref[t] = product
        out_ref[t] = product.astype(bf16)
        return carry

    lax.fori_loop(0, half, base, 0, unroll=half)

    def more(t, carry):
        place = more_ids_ref[t] - part * half

        @pl.when((place >= 0) & (place < half))
        def _():
            total = acc_ref[place] + grouped_product(tiles_ref, ids_ref, panel_ref, more_ref, t)
            acc_ref[place] = total
            out_ref[place] = total.astype(bf16)

        return carry

    lax.fori_loop(0, total_ref[0], more, 0)


def forward_tiles(part, lists, panel, tiles):
    block, width = panel.shape[1:]
    shape = (lists[0].shape[0] // (2 * quad), block, width)
    return pl.pallas_call(
        functools.partial(forward_kernel, part),
        out_shape=jax.ShapeDtypeStruct(shape, bf16),
        in_specs=[smem] * 5 + [vmem] * 2,
        out_specs=vmem,
        scratch_shapes=[pltpu.VMEM(shape, f32)],
        compiler_params=params(),
        cost_estimate=cost(2 * shape[0] * quad * block * block * width, tiles.size),
        name="forward_tiles_%d" % part,
    )(*lists, panel, tiles)


def spread_kernel(in_ref, out_ref):
    for k in range(out_ref.shape[0]):
        out_ref[k] = in_ref[...]


def spread(shard, copies):
    return pl.pallas_call(
        spread_kernel,
        out_shape=pltpu.VMEM((copies,) + shard.shape, shard.dtype),
        in_specs=[vmem],
        out_specs=vmem,
        compiler_params=params(),
        name="spread",
    )(shard)


def sum_parts(ref):
    total = ref[0].astype(f32)
    for k in range(1, ref.shape[0]):
        total += ref[k].astype(f32)
    return total


def dense_kernel(parts_ref, weight_ref, cotangent_ref, act_ref, message_ref):
    aggregated = sum_parts(parts_ref)
    aggregated_half = aggregated.astype(bf16)
    preact = jnp.dot(aggregated_half, weight_ref[...], preferred_element_type=f32)
    scale = math.sqrt(2 / math.pi)
    square = preact * preact
    tanh = jnp.tanh(scale * (preact + 0.044715 * (square * preact)))
    act_ref[...] = (0.5 * preact * (1.0 + tanh)).astype(bf16)
    slope = 0.5 * (1.0 + tanh) + (0.5 * preact) * (1.0 - tanh * tanh) * (
        scale * (1.0 + (3 * 0.044715) * square)
    )
    grad_pre = (cotangent_ref[...].astype(f32) * slope).astype(bf16)
    turned = aggregated_half.astype(f32).T
    peers = message_ref.shape[0]
    rows = grad_pre.shape[0]
    own = 2 * turned.shape[0] // peers
    for k in range(peers):
        message_ref[k, :rows, :] = grad_pre
        first = (k // 2) * own
        low = turned[first : first + own // 2]
        high = turned[first + own // 2 : first + own]
        message_ref[k, rows:, :] = jnp.concatenate([low, high], axis=1).astype(bf16)


def dense(parts, weight, cotangent):
    rows, width = cotangent.shape
    peers = parts.shape[0]
    return pl.pallas_call(
        dense_kernel,
        out_shape=(
            jax.ShapeDtypeStruct((rows, width), bf16),
            jax.ShapeDtypeStruct((peers, rows + width // peers, width), bf16),
        ),
        in_specs=[vmem] * 3,
        out_specs=(vmem,) * 2,
        compiler_params=params(),
        name="dense",
    )(parts, weight, cotangent)


def weight_kernel(mine_ref, out_ref):
    peers, _, width = mine_ref.shape
    rows = width // 2
    total = None
    for k in range(0, peers, 2):
        left = []
        for p in (k, k + 1):
            packed = mine_ref[p, rows:, :].astype(f32)
            left.append(jnp.concatenate([packed[:, :rows], packed[:, rows:]], axis=0))
        left = jnp.concatenate(left, axis=1).astype(bf16)
        right = jnp.concatenate([mine_ref[k, :rows, :], mine_ref[k + 1, :rows, :]], axis=0)
        term = jnp.dot(left, right, preferred_element_type=f32)
        total = term if total is None else total + term
    rounded = total.astype(bf16)
    for k in range(out_ref.shape[0]):
        out_ref[k] = rounded


def weight_part(mine, copies):
    peers, _, width = mine.shape
    return pl.pallas_call(
        weight_kernel,
        out_shape=jax.ShapeDtypeStruct((copies, 2 * width // peers, width), bf16),
        in_specs=[vmem],
        out_specs=vmem,
        compiler_params=params(),
        cost_estimate=cost(0, mine.size),
        name="weight_part",
    )(mine)


def weight_sum_kernel(scale, parts_ref, out_ref):
    out_ref[...] = sum_parts(parts_ref) * scale


def weight_sum(parts, scale):
    return pl.pallas_call(
        functools.partial(weight_sum_kernel, scale),
        out_shape=jax.ShapeDtypeStruct(parts.shape[1:], f32),
        in_specs=[vmem],
        out_specs=vmem,
        compiler_params=params(),
        cost_estimate=cost(0, parts.size),
        name="weight_sum",
    )(parts)


def gather_over_col(rows, position, size):
    held = (rows + lax.ppermute(rows, "col", [(i, i ^ 1) for i in range(size)]))[None]
    steps = (size // 2, size // 4, size // 8)
    for distance in steps:
        came = lax.ppermute(held, "col", [(i, i ^ distance) for i in range(size)])
        if distance == steps[-1]:
            return held, came
        upper = (position // distance) % 2 == 1
        held = jnp.where(upper, jnp.concatenate([came, held]), jnp.concatenate([held, came]))


def backward_kernel(*refs):
    *refs, held_ref, held_sem = refs
    tiles_copy = pltpu.make_async_copy(refs[7], held_ref, held_sem)
    tiles_copy.start()
    tiles_copy.wait()
    lists = refs[:5]
    list_ref, more_ref, more_ids_ref, total_ref, ids_ref = lists
    mine_ref, other_ref, _, out_ref, acc_ref = refs[5:]
    tiles_ref = held_ref
    targets = out_ref.shape[0]

    def base(t, carry):
        product = grouped_product(tiles_ref, ids_ref, mine_ref, list_ref, t)
        product += grouped_product(tiles_ref, ids_ref, other_ref, list_ref, targets + t)
        acc_ref[t] = product
        out_ref[t] = product.astype(bf16)
        return carry

    lax.fori_loop(0, targets, base, 0, unroll=targets)

    def more(t, carry):
        target = more_ids_ref[t]
        place = target % targets

        @pl.when(target < targets)
        def _():
            acc_ref[place] += grouped_product(tiles_ref, ids_ref, mine_ref, more_ref, t)

        @pl.when(target >= targets)
        def _():
            acc_ref[place] += grouped_product(tiles_ref, ids_ref, other_ref, more_ref, t)

        out_ref[place] = acc_ref[place].astype(bf16)
        return carry

    lax.fori_loop(0, total_ref[0], more, 0)


def backward_tiles(lists, mine, other, tiles):
    width = mine.shape[-1]
    block = tiles.shape[-1]
    shape = (lists[0].shape[0] // (2 * quad), block, width)
    return pl.pallas_call(
        backward_kernel,
        out_shape=jax.ShapeDtypeStruct(shape, bf16),
        in_specs=[smem] * 5 + [vmem] * 2 + [pl.BlockSpec(memory_space=pltpu.HBM)],
        out_specs=vmem,
        scratch_shapes=[pltpu.VMEM(shape, f32), pltpu.VMEM(tiles.shape, bf16), pltpu.SemaphoreType.DMA],
        compiler_params=params(),
        cost_estimate=cost(4 * shape[0] * quad * block * block * width, tiles.size),
        name="backward_tiles",
    )(*lists, mine, other, pltpu.with_memory_space_constraint(tiles, pltpu.HBM))


def finish_kernel(upper_ref, parts_ref, weight_ref, held_ref, came_ref, out_ref, weight_out_ref):
    out_ref[...] = lax.dot_general(
        sum_parts(parts_ref).astype(bf16), weight_ref[...], (((1,), (1,)), ((), ())), preferred_element_type=f32
    ).astype(bf16)
    upper = upper_ref[0] == 1
    chunks, own, _ = held_ref.shape
    for k in range(2 * chunks):
        bits = [(k >> b) & 1 for b in range(3)]
        place = bits[1] * 2 + bits[2]
        held, came = held_ref[place], came_ref[place]
        low, high = (held, came) if bits[0] == 0 else (came, held)
        weight_out_ref[k * own : (k + 1) * own, :] = jnp.where(upper, high, low)


def finish(upper, parts, weight, held, came):
    return pl.pallas_call(
        finish_kernel,
        out_shape=(jax.ShapeDtypeStruct(parts.shape[1:], bf16), jax.ShapeDtypeStruct(weight.shape, f32)),
        in_specs=[smem] + [vmem] * 4,
        out_specs=(vmem,) * 2,
        compiler_params=params(),
        name="finish",
    )(upper, parts, weight, held, came)


def local(features, weight, block_values, block_rows, block_cols, counts, cotangent):
    rows_dev, width = features.shape
    row_count = lax.axis_size("row")
    col_count = lax.axis_size("col")
    node_total = rows_dev * row_count * col_count
    half = col_count // 2
    pairs = [(i, i ^ 1) for i in range(col_count)]
    groups = [[2 * k + c for k in range(half)] for c in range(2)]
    position = lax.axis_index("col").astype(i32)
    core = jnp.reshape(position % 2, (1,))
    tiles = block_values[0, 0]

    panel = lax.all_to_all(spread(features, row_count), "row", 0, 0)
    made = prepare(block_rows[0, 0], block_cols[0, 0], counts[0], core, tiles, col_count)
    forward_lists, (*backward_lists, backward_ids), flipped = made[:5], made[5:10], made[10]

    send = forward_tiles(1, forward_lists, panel, tiles)
    came = lax.ppermute(send, "col", pairs)
    keep = forward_tiles(0, forward_lists, panel, tiles)
    summed = (keep.astype(f32) + came.astype(f32)).astype(bf16)
    parts = lax.all_to_all(summed, "col", 0, 0, axis_index_groups=groups)
    activations, messages = dense(parts, weight, cotangent)

    mine = lax.all_to_all(messages, "col", 0, 0, axis_index_groups=groups)
    other = lax.ppermute(mine, "col", pairs)
    weight_rows, backward_ids = lax.optimization_barrier((weight_part(mine, row_count), backward_ids))
    weight_parts = lax.all_to_all(weight_rows, "row", 0, 0)
    back = backward_tiles((*backward_lists, backward_ids), mine, other, flipped)
    back_parts = lax.all_to_all(back, "row", 0, 0)
    weight_rows = weight_sum(weight_parts, 1.0 / math.sqrt(node_total))
    held, came = gather_over_col(weight_rows, position, col_count)
    upper = jnp.reshape((position // (col_count // 8)) % 2, (1,))
    feature_grad, weight_grad = finish(upper, back_parts, weight, held, came)
    return (activations, feature_grad, weight_grad)


def solution(mesh):
    in_specs = (
        P(("col", "row"), None),
        P(),
        P("row", "col", None, None, None),
        P("row", "col", None),
        P("row", "col", None),
        P("row", "col"),
        P(("row", "col"), None),
    )
    out_specs = (P(("row", "col"), None), P(("col", "row"), None), P())
    return jax.shard_map(local, mesh=mesh, in_specs=in_specs, out_specs=out_specs, check_vma=False)
```

```python
import functools
import math

import jax
import jax.numpy as jnp
from jax import lax
from jax.experimental import pallas as pl
from jax.experimental.pallas import tpu as pltpu
from jax.sharding import PartitionSpec as P

bf16 = jnp.bfloat16
f32 = jnp.float32
i32 = jnp.int32
smem = pl.BlockSpec(memory_space=pltpu.SMEM)
vmem = pl.BlockSpec(memory_space=pltpu.VMEM)
quad = 4


def params(mib=16):
    return pltpu.CompilerParams(vmem_limit_bytes=mib * 1024 * 1024)


def cost(flops, moved):
    return pl.CostEstimate(flops=flops, bytes_accessed=moved, transcendentals=0)


def sort_slots(target_of, slots, count, base_ref, extra_ref, extra_ids_ref, total_ref, seen_ref, last_ref):
    zero_slot = slots
    size = quad
    targets = base_ref.shape[0] // size

    def clear_base(t, carry):
        base_ref[t] = zero_slot
        return carry

    def clear_extra(t, carry):
        extra_ref[t] = zero_slot
        return carry

    def clear_seen(t, carry):
        seen_ref[t] = 0
        return carry

    lax.fori_loop(0, base_ref.shape[0], clear_base, 0)
    lax.fori_loop(0, extra_ref.shape[0], clear_extra, 0)
    lax.fori_loop(0, targets, clear_seen, 0)
    total_ref[0] = 0

    def place(s, carry):
        target = target_of(s)
        seen = seen_ref[target]
        seen_ref[target] = seen + 1

        @pl.when(seen < size)
        def _():
            base_ref[target * size + seen] = s

        @pl.when(seen >= size)
        def _():
            over = seen % size

            @pl.when(over == 0)
            def _():
                group = total_ref[0]
                total_ref[0] = group + 1
                last_ref[target] = group
                extra_ids_ref[group] = target

            extra_ref[last_ref[target] * size + over] = s

        return carry

    lax.fori_loop(0, count, place, 0)


def prepare_kernel(
    rows_ref, cols_ref, count_ref, core_ref, tiles_ref,
    fwd_ref, fwd_more_ref, fwd_more_ids_ref, fwd_total_ref, fwd_source_ref,
    bwd_ref, bwd_more_ref, bwd_more_ids_ref, bwd_total_ref, bwd_source_ref,
    flipped_ref, seen_ref, last_ref,
):
    slots = rows_ref.shape[0]
    count = count_ref[0]
    core = core_ref[0]
    half = fwd_ref.shape[0] // (2 * quad)

    def away(s):
        return (rows_ref[s] % 2 != core).astype(i32)

    def place(s):
        return (rows_ref[s] // 2 % 2) * (half // 2) + rows_ref[s] // 4

    def forward_target(s):
        return away(s) * half + place(s)

    def backward_target(s):
        return away(s) * half + cols_ref[s]

    sort_slots(forward_target, slots, count, fwd_ref, fwd_more_ref, fwd_more_ids_ref, fwd_total_ref, seen_ref, last_ref)
    sort_slots(backward_target, slots, count, bwd_ref, bwd_more_ref, bwd_more_ids_ref, bwd_total_ref, seen_ref, last_ref)

    def sources(s, carry):
        fwd_source_ref[s] = cols_ref[s]
        bwd_source_ref[s] = place(s)
        return carry

    lax.fori_loop(0, slots, sources, 0)
    fwd_source_ref[slots] = 0
    bwd_source_ref[slots] = 0

    def turn(s, carry):
        flipped_ref[s] = tiles_ref[s].T
        return carry

    lax.fori_loop(0, slots, turn, 0, unroll=4)
    flipped_ref[slots] = jnp.zeros(flipped_ref.shape[1:], bf16)


def prepare(rows_ids, cols_ids, count, core, tiles, targets):
    slots, block, _ = tiles.shape
    ints = lambda size: jax.ShapeDtypeStruct((size,), i32)
    held = jax.ShapeDtypeStruct((slots + 1, block, block), bf16)
    lists = (ints(targets * quad), ints(slots * quad), ints(slots), ints(1), ints(slots + 1))
    return pl.pallas_call(
        prepare_kernel,
        out_shape=(*lists, *lists, held),
        in_specs=[smem] * 4 + [vmem],
        out_specs=(smem,) * 10 + (vmem,),
        scratch_shapes=[pltpu.SMEM((targets,), i32)] * 2,
        compiler_params=params(24),
        cost_estimate=cost(0, 9 * slots * block * block * 2),
        name="prepare",
    )(rows_ids, cols_ids, count, core, tiles)


def grouped_product(tiles_ref, ids_ref, source_ref, list_ref, group):
    slots = [list_ref[group * quad + k] for k in range(quad)]
    block = tiles_ref.shape[1]
    held = tiles_ref.shape[0]
    if held == ids_ref.shape[0]:
        parts = [tiles_ref[s] for s in slots]
    else:
        parts = [tiles_ref[jnp.minimum(s, held - 1)] for s in slots]
        parts = [jnp.where(s < held, part, jnp.zeros_like(part)) for s, part in zip(slots, parts)]
    left = jnp.concatenate(parts, axis=1)
    right = jnp.concatenate([source_ref[ids_ref[s], :block, :] for s in slots], axis=0)
    return jnp.dot(left, right, preferred_element_type=f32)


def forward_kernel(part, *refs):
    lists = refs[:5]
    list_ref, more_ref, more_ids_ref, total_ref, ids_ref = lists
    panel_ref, tiles_ref, out_ref, acc_ref = refs[5:]
    half = out_ref.shape[0]

    def base(t, carry):
        product = grouped_product(tiles_ref, ids_ref, panel_ref, list_ref, part * half + t)
        acc_ref[t] = product
        out_ref[t] = product.astype(bf16)
        return carry

    lax.fori_loop(0, half, base, 0, unroll=half)

    def more(t, carry):
        place = more_ids_ref[t] - part * half

        @pl.when((place >= 0) & (place < half))
        def _():
            total = acc_ref[place] + grouped_product(tiles_ref, ids_ref, panel_ref, more_ref, t)
            acc_ref[place] = total
            out_ref[place] = total.astype(bf16)

        return carry

    lax.fori_loop(0, total_ref[0], more, 0)


def forward_tiles(part, lists, panel, tiles):
    block, width = panel.shape[1:]
    shape = (lists[0].shape[0] // (2 * quad), block, width)
    return pl.pallas_call(
        functools.partial(forward_kernel, part),
        out_shape=jax.ShapeDtypeStruct(shape, bf16),
        in_specs=[smem] * 5 + [vmem] * 2,
        out_specs=vmem,
        scratch_shapes=[pltpu.VMEM(shape, f32)],
        compiler_params=params(),
        cost_estimate=cost(2 * shape[0] * quad * block * block * width, tiles.size),
        name="forward_tiles_%d" % part,
    )(*lists, panel, tiles)


def spread_kernel(in_ref, out_ref):
    for k in range(out_ref.shape[0]):
        out_ref[k] = in_ref[...]


def spread(shard, copies):
    return pl.pallas_call(
        spread_kernel,
        out_shape=pltpu.VMEM((copies,) + shard.shape, shard.dtype),
        in_specs=[vmem],
        out_specs=vmem,
        compiler_params=params(),
        name="spread",
    )(shard)


def sum_parts(ref):
    total = ref[0].astype(f32)
    for k in range(1, ref.shape[0]):
        total += ref[k].astype(f32)
    return total


def dense_kernel(parts_ref, weight_ref, cotangent_ref, act_ref, message_ref):
    aggregated = sum_parts(parts_ref)
    aggregated_half = aggregated.astype(bf16)
    preact = jnp.dot(aggregated_half, weight_ref[...], preferred_element_type=f32)
    scale = math.sqrt(2 / math.pi)
    square = preact * preact
    tanh = jnp.tanh(scale * (preact + 0.044715 * (square * preact)))
    act_ref[...] = (0.5 * preact * (1.0 + tanh)).astype(bf16)
    slope = 0.5 * (1.0 + tanh) + (0.5 * preact) * (1.0 - tanh * tanh) * (
        scale * (1.0 + (3 * 0.044715) * square)
    )
    grad_pre = (cotangent_ref[...].astype(f32) * slope).astype(bf16)
    turned = aggregated_half.astype(f32).T
    peers = message_ref.shape[0]
    rows = grad_pre.shape[0]
    own = 2 * turned.shape[0] // peers
    for k in range(peers):
        message_ref[k, :rows, :] = grad_pre
        first = (k % (peers // 2)) * own
        low = turned[first : first + own // 2]
        high = turned[first + own // 2 : first + own]
        message_ref[k, rows:, :] = jnp.concatenate([low, high], axis=1).astype(bf16)


def dense(parts, weight, cotangent):
    rows, width = cotangent.shape
    peers = parts.shape[0]
    return pl.pallas_call(
        dense_kernel,
        out_shape=(
            jax.ShapeDtypeStruct((rows, width), bf16),
            jax.ShapeDtypeStruct((peers, rows + width // peers, width), bf16),
        ),
        in_specs=[vmem] * 3,
        out_specs=(vmem,) * 2,
        compiler_params=params(),
        name="dense",
    )(parts, weight, cotangent)


def weight_kernel(mine_ref, out_ref):
    peers, _, width = mine_ref.shape
    rows = width // 2
    total = None
    for k in range(0, peers, 2):
        left = []
        for p in (k, k + 1):
            packed = mine_ref[p, rows:, :].astype(f32)
            left.append(jnp.concatenate([packed[:, :rows], packed[:, rows:]], axis=0))
        left = jnp.concatenate(left, axis=1).astype(bf16)
        right = jnp.concatenate([mine_ref[k, :rows, :], mine_ref[k + 1, :rows, :]], axis=0)
        term = jnp.dot(left, right, preferred_element_type=f32)
        total = term if total is None else total + term
    rounded = total.astype(bf16)
    for k in range(out_ref.shape[0]):
        out_ref[k] = rounded


def weight_part(mine, copies):
    peers, _, width = mine.shape
    return pl.pallas_call(
        weight_kernel,
        out_shape=jax.ShapeDtypeStruct((copies, 2 * width // peers, width), bf16),
        in_specs=[vmem],
        out_specs=vmem,
        compiler_params=params(),
        cost_estimate=cost(0, mine.size),
        name="weight_part",
    )(mine)


def weight_sum_kernel(scale, parts_ref, out_ref):
    out_ref[...] = sum_parts(parts_ref) * scale


def weight_sum(parts, scale):
    return pl.pallas_call(
        functools.partial(weight_sum_kernel, scale),
        out_shape=jax.ShapeDtypeStruct(parts.shape[1:], f32),
        in_specs=[vmem],
        out_specs=vmem,
        compiler_params=params(),
        cost_estimate=cost(0, parts.size),
        name="weight_sum",
    )(parts)


def gather_over_col(rows, position, size):
    held = (rows + lax.ppermute(rows, "col", [(i, i ^ 1) for i in range(size)]))[None]
    steps = (size // 2, size // 4, size // 8)
    for distance in steps:
        came = lax.ppermute(held, "col", [(i, i ^ distance) for i in range(size)])
        if distance == steps[-1]:
            return held, came
        upper = (position // distance) % 2 == 1
        held = jnp.where(upper, jnp.concatenate([came, held]), jnp.concatenate([held, came]))


def backward_kernel(*refs):
    *refs, held_ref, held_sem = refs
    tiles_copy = pltpu.make_async_copy(refs[7], held_ref, held_sem)
    tiles_copy.start()
    tiles_copy.wait()
    lists = refs[:5]
    list_ref, more_ref, more_ids_ref, total_ref, ids_ref = lists
    mine_ref, other_ref, _, out_ref, acc_ref = refs[5:]
    tiles_ref = held_ref
    targets = out_ref.shape[0]

    def base(t, carry):
        product = grouped_product(tiles_ref, ids_ref, mine_ref, list_ref, t)
        product += grouped_product(tiles_ref, ids_ref, other_ref, list_ref, targets + t)
        acc_ref[t] = product
        out_ref[t] = product.astype(bf16)
        return carry

    lax.fori_loop(0, targets, base, 0, unroll=targets)

    def more(t, carry):
        target = more_ids_ref[t]
        place = target % targets

        @pl.when(target < targets)
        def _():
            acc_ref[place] += grouped_product(tiles_ref, ids_ref, mine_ref, more_ref, t)

        @pl.when(target >= targets)
        def _():
            acc_ref[place] += grouped_product(tiles_ref, ids_ref, other_ref, more_ref, t)

        out_ref[place] = acc_ref[place].astype(bf16)
        return carry

    lax.fori_loop(0, total_ref[0], more, 0)


def backward_tiles(lists, mine, other, tiles):
    width = mine.shape[-1]
    block = tiles.shape[-1]
    shape = (lists[0].shape[0] // (2 * quad), block, width)
    return pl.pallas_call(
        backward_kernel,
        out_shape=jax.ShapeDtypeStruct(shape, bf16),
        in_specs=[smem] * 5 + [vmem] * 2 + [pl.BlockSpec(memory_space=pltpu.HBM)],
        out_specs=vmem,
        scratch_shapes=[pltpu.VMEM(shape, f32), pltpu.VMEM(tiles.shape, bf16), pltpu.SemaphoreType.DMA],
        compiler_params=params(),
        cost_estimate=cost(4 * shape[0] * quad * block * block * width, tiles.size),
        name="backward_tiles",
    )(*lists, mine, other, pltpu.with_memory_space_constraint(tiles, pltpu.HBM))


def finish_kernel(upper_ref, parts_ref, weight_ref, held_ref, came_ref, out_ref, weight_out_ref):
    out_ref[...] = lax.dot_general(
        sum_parts(parts_ref).astype(bf16), weight_ref[...], (((1,), (1,)), ((), ())), preferred_element_type=f32
    ).astype(bf16)
    upper = upper_ref[0] == 1
    chunks, own, _ = held_ref.shape
    for k in range(2 * chunks):
        bits = [(k >> b) & 1 for b in range(3)]
        place = bits[1] * 2 + bits[2]
        held, came = held_ref[place], came_ref[place]
        low, high = (held, came) if bits[0] == 0 else (came, held)
        weight_out_ref[k * own : (k + 1) * own, :] = jnp.where(upper, high, low)


def finish(upper, parts, weight, held, came):
    return pl.pallas_call(
        finish_kernel,
        out_shape=(jax.ShapeDtypeStruct(parts.shape[1:], bf16), jax.ShapeDtypeStruct(weight.shape, f32)),
        in_specs=[smem] + [vmem] * 4,
        out_specs=(vmem,) * 2,
        compiler_params=params(),
        name="finish",
    )(upper, parts, weight, held, came)


def local(features, weight, block_values, block_rows, block_cols, counts, cotangent):
    rows_dev, width = features.shape
    row_count = lax.axis_size("row")
    col_count = lax.axis_size("col")
    node_total = rows_dev * row_count * col_count
    half = col_count // 2
    pairs = [(i, i ^ 1) for i in range(col_count)]
    groups = [[4 * y + 2 * x + c for x in range(2) for y in range(half // 2)] for c in range(2)]
    position = lax.axis_index("col").astype(i32)
    core = jnp.reshape(position % 2, (1,))
    tiles = block_values[0, 0]

    panel = lax.all_to_all(spread(features, row_count), "row", 0, 0)
    made = prepare(block_rows[0, 0], block_cols[0, 0], counts[0], core, tiles, col_count)
    forward_lists, (*backward_lists, backward_ids), flipped = made[:5], made[5:10], made[10]

    send = forward_tiles(1, forward_lists, panel, tiles)
    came = lax.ppermute(send, "col", pairs)
    keep = forward_tiles(0, forward_lists, panel, tiles)
    summed = (keep.astype(f32) + came.astype(f32)).astype(bf16)
    parts = lax.all_to_all(summed, "col", 0, 0, axis_index_groups=groups)
    activations, messages = dense(parts, weight, cotangent)

    mine = lax.all_to_all(messages, "col", 0, 0, axis_index_groups=groups)
    other = lax.ppermute(mine, "col", pairs)
    weight_rows, backward_ids = lax.optimization_barrier((weight_part(mine, row_count), backward_ids))
    weight_parts = lax.all_to_all(weight_rows, "row", 0, 0)
    back = backward_tiles((*backward_lists, backward_ids), mine, other, flipped)
    back_parts = lax.all_to_all(back, "row", 0, 0)
    weight_rows = weight_sum(weight_parts, 1.0 / math.sqrt(node_total))
    held, came = gather_over_col(weight_rows, position, col_count)
    upper = jnp.reshape((position // (col_count // 8)) % 2, (1,))
    feature_grad, weight_grad = finish(upper, back_parts, weight, held, came)
    return (activations, feature_grad, weight_grad)


def solution(mesh):
    in_specs = (
        P(("col", "row"), None),
        P(),
        P("row", "col", None, None, None),
        P("row", "col", None),
        P("row", "col", None),
        P("row", "col"),
        P(("row", "col"), None),
    )
    out_specs = (P(("row", "col"), None), P(("col", "row"), None), P())
    return jax.shard_map(local, mesh=mesh, in_specs=in_specs, out_specs=out_specs, check_vma=False)
```

```python
import functools
import math

import jax
import jax.numpy as jnp
from jax import lax
from jax.experimental import pallas as pl
from jax.experimental.pallas import tpu as pltpu
from jax.sharding import PartitionSpec as P

bf16 = jnp.bfloat16
f32 = jnp.float32
i32 = jnp.int32
smem = pl.BlockSpec(memory_space=pltpu.SMEM)
vmem = pl.BlockSpec(memory_space=pltpu.VMEM)
quad = 4


def params(mib=16):
    return pltpu.CompilerParams(vmem_limit_bytes=mib * 1024 * 1024)


def cost(flops, moved):
    return pl.CostEstimate(flops=flops, bytes_accessed=moved, transcendentals=0)


def sort_slots(target_of, slots, count, base_ref, extra_ref, extra_ids_ref, total_ref, seen_ref, last_ref):
    zero_slot = slots
    size = quad
    targets = base_ref.shape[0] // size

    def clear_base(t, carry):
        base_ref[t] = zero_slot
        return carry

    def clear_extra(t, carry):
        extra_ref[t] = zero_slot
        return carry

    def clear_seen(t, carry):
        seen_ref[t] = 0
        return carry

    lax.fori_loop(0, base_ref.shape[0], clear_base, 0)
    lax.fori_loop(0, extra_ref.shape[0], clear_extra, 0)
    lax.fori_loop(0, targets, clear_seen, 0)
    total_ref[0] = 0

    def place(s, carry):
        target = target_of(s)
        seen = seen_ref[target]
        seen_ref[target] = seen + 1

        @pl.when(seen < size)
        def _():
            base_ref[target * size + seen] = s

        @pl.when(seen >= size)
        def _():
            over = seen % size

            @pl.when(over == 0)
            def _():
                group = total_ref[0]
                total_ref[0] = group + 1
                last_ref[target] = group
                extra_ids_ref[group] = target

            extra_ref[last_ref[target] * size + over] = s

        return carry

    lax.fori_loop(0, count, place, 0)


def prepare_kernel(
    rows_ref, cols_ref, count_ref, core_ref, tiles_ref,
    fwd_ref, fwd_more_ref, fwd_more_ids_ref, fwd_total_ref, fwd_source_ref,
    bwd_ref, bwd_more_ref, bwd_more_ids_ref, bwd_total_ref, bwd_source_ref,
    flipped_ref, seen_ref, last_ref,
):
    slots = rows_ref.shape[0]
    count = count_ref[0]
    core = core_ref[0]
    half = fwd_ref.shape[0] // (2 * quad)

    def away(s):
        return (rows_ref[s] % 2 != core).astype(i32)

    def place(s):
        return (rows_ref[s] // 2 % 2) * (half // 2) + rows_ref[s] // 4

    def forward_target(s):
        return away(s) * half + place(s)

    def backward_target(s):
        return away(s) * half + cols_ref[s]

    sort_slots(forward_target, slots, count, fwd_ref, fwd_more_ref, fwd_more_ids_ref, fwd_total_ref, seen_ref, last_ref)
    sort_slots(backward_target, slots, count, bwd_ref, bwd_more_ref, bwd_more_ids_ref, bwd_total_ref, seen_ref, last_ref)

    def sources(s, carry):
        fwd_source_ref[s] = cols_ref[s]
        bwd_source_ref[s] = place(s)
        return carry

    lax.fori_loop(0, slots, sources, 0)
    fwd_source_ref[slots] = 0
    bwd_source_ref[slots] = 0

    def turn(s, carry):
        flipped_ref[s] = tiles_ref[s].T
        return carry

    lax.fori_loop(0, slots, turn, 0, unroll=4)
    flipped_ref[slots] = jnp.zeros(flipped_ref.shape[1:], bf16)


def prepare(rows_ids, cols_ids, count, core, tiles, targets):
    slots, block, _ = tiles.shape
    ints = lambda size: jax.ShapeDtypeStruct((size,), i32)
    held = jax.ShapeDtypeStruct((slots + 1, block, block), bf16)
    lists = (ints(targets * quad), ints(slots * quad), ints(slots), ints(1), ints(slots + 1))
    return pl.pallas_call(
        prepare_kernel,
        out_shape=(*lists, *lists, held),
        in_specs=[smem] * 4 + [vmem],
        out_specs=(smem,) * 10 + (vmem,),
        scratch_shapes=[pltpu.SMEM((targets,), i32)] * 2,
        compiler_params=params(24),
        cost_estimate=cost(0, 9 * slots * block * block * 2),
        name="prepare",
    )(rows_ids, cols_ids, count, core, tiles)


def grouped_product(tiles_ref, ids_ref, source_ref, list_ref, group):
    slots = [list_ref[group * quad + k] for k in range(quad)]
    block = tiles_ref.shape[1]
    held = tiles_ref.shape[0]
    if held == ids_ref.shape[0]:
        parts = [tiles_ref[s] for s in slots]
    else:
        parts = [tiles_ref[jnp.minimum(s, held - 1)] for s in slots]
        parts = [jnp.where(s < held, part, jnp.zeros_like(part)) for s, part in zip(slots, parts)]
    left = jnp.concatenate(parts, axis=1)
    right = jnp.concatenate([source_ref[ids_ref[s], :block, :] for s in slots], axis=0)
    return jnp.dot(left, right, preferred_element_type=f32)


def forward_kernel(part, *refs):
    lists = refs[:5]
    list_ref, more_ref, more_ids_ref, total_ref, ids_ref = lists
    panel_ref, tiles_ref, out_ref, acc_ref = refs[5:]
    half = out_ref.shape[0]

    def base(t, carry):
        product = grouped_product(tiles_ref, ids_ref, panel_ref, list_ref, part * half + t)
        acc_ref[t] = product
        out_ref[t] = product.astype(bf16)
        return carry

    lax.fori_loop(0, half, base, 0, unroll=half)

    def more(t, carry):
        place = more_ids_ref[t] - part * half

        @pl.when((place >= 0) & (place < half))
        def _():
            total = acc_ref[place] + grouped_product(tiles_ref, ids_ref, panel_ref, more_ref, t)
            acc_ref[place] = total
            out_ref[place] = total.astype(bf16)

        return carry

    lax.fori_loop(0, total_ref[0], more, 0)


def forward_tiles(part, lists, panel, tiles):
    block, width = panel.shape[1:]
    shape = (lists[0].shape[0] // (2 * quad), block, width)
    return pl.pallas_call(
        functools.partial(forward_kernel, part),
        out_shape=jax.ShapeDtypeStruct(shape, bf16),
        in_specs=[smem] * 5 + [vmem] * 2,
        out_specs=vmem,
        scratch_shapes=[pltpu.VMEM(shape, f32)],
        compiler_params=params(),
        cost_estimate=cost(2 * shape[0] * quad * block * block * width, tiles.size),
        name="forward_tiles_%d" % part,
    )(*lists, panel, tiles)


def spread_kernel(in_ref, out_ref):
    for k in range(out_ref.shape[0]):
        out_ref[k] = in_ref[...]


def spread(shard, copies):
    return pl.pallas_call(
        spread_kernel,
        out_shape=pltpu.VMEM((copies,) + shard.shape, shard.dtype),
        in_specs=[vmem],
        out_specs=vmem,
        compiler_params=params(),
        name="spread",
    )(shard)


def sum_parts(ref):
    total = ref[0].astype(f32)
    for k in range(1, ref.shape[0]):
        total += ref[k].astype(f32)
    return total


def dense_kernel(parts_ref, weight_ref, cotangent_ref, act_ref, message_ref):
    aggregated = sum_parts(parts_ref)
    aggregated_half = aggregated.astype(bf16)
    preact = jnp.dot(aggregated_half, weight_ref[...], preferred_element_type=f32)
    scale = math.sqrt(2 / math.pi)
    square = preact * preact
    tanh = jnp.tanh(scale * (preact + 0.044715 * (square * preact)))
    act_ref[...] = (0.5 * preact * (1.0 + tanh)).astype(bf16)
    slope = 0.5 * (1.0 + tanh) + (0.5 * preact) * (1.0 - tanh * tanh) * (
        scale * (1.0 + (3 * 0.044715) * square)
    )
    grad_pre = (cotangent_ref[...].astype(f32) * slope).astype(bf16)
    turned = aggregated_half.astype(f32).T
    peers = message_ref.shape[0]
    rows = grad_pre.shape[0]
    own = 2 * turned.shape[0] // peers
    for k in range(peers):
        message_ref[k, :rows, :] = grad_pre
        first = (k % (peers // 2)) * own
        low = turned[first : first + own // 2]
        high = turned[first + own // 2 : first + own]
        message_ref[k, rows:, :] = jnp.concatenate([low, high], axis=1).astype(bf16)


def dense(parts, weight, cotangent):
    rows, width = cotangent.shape
    peers = parts.shape[0]
    return pl.pallas_call(
        dense_kernel,
        out_shape=(
            jax.ShapeDtypeStruct((rows, width), bf16),
            jax.ShapeDtypeStruct((peers, rows + width // peers, width), bf16),
        ),
        in_specs=[vmem] * 3,
        out_specs=(vmem,) * 2,
        compiler_params=params(),
        name="dense",
    )(parts, weight, cotangent)


def weight_kernel(mine_ref, out_ref):
    peers, _, width = mine_ref.shape
    rows = width // 2
    total = None
    for k in range(0, peers, 2):
        left = []
        for p in (k, k + 1):
            packed = mine_ref[p, rows:, :].astype(f32)
            left.append(jnp.concatenate([packed[:, :rows], packed[:, rows:]], axis=0))
        left = jnp.concatenate(left, axis=1).astype(bf16)
        right = jnp.concatenate([mine_ref[k, :rows, :], mine_ref[k + 1, :rows, :]], axis=0)
        term = jnp.dot(left, right, preferred_element_type=f32)
        total = term if total is None else total + term
    rounded = total.astype(bf16)
    for k in range(out_ref.shape[0]):
        out_ref[k] = rounded


def weight_part(mine, copies):
    peers, _, width = mine.shape
    return pl.pallas_call(
        weight_kernel,
        out_shape=jax.ShapeDtypeStruct((copies, 2 * width // peers, width), bf16),
        in_specs=[vmem],
        out_specs=vmem,
        compiler_params=params(),
        cost_estimate=cost(0, mine.size),
        name="weight_part",
    )(mine)


def weight_sum_kernel(scale, parts_ref, out_ref):
    out_ref[...] = sum_parts(parts_ref) * scale


def weight_sum(parts, scale):
    return pl.pallas_call(
        functools.partial(weight_sum_kernel, scale),
        out_shape=jax.ShapeDtypeStruct(parts.shape[1:], f32),
        in_specs=[vmem],
        out_specs=vmem,
        compiler_params=params(),
        cost_estimate=cost(0, parts.size),
        name="weight_sum",
    )(parts)


def gather_over_col(rows, position, size):
    held = (rows + lax.ppermute(rows, "col", [(i, i ^ 1) for i in range(size)])).astype(bf16)[None]
    steps = (size // 2, size // 4, size // 8)
    for distance in steps:
        came = lax.ppermute(held, "col", [(i, i ^ distance) for i in range(size)])
        if distance == steps[-1]:
            return held, came
        upper = (position // distance) % 2 == 1
        held = jnp.where(upper, jnp.concatenate([came, held]), jnp.concatenate([held, came]))


def backward_kernel(*refs):
    *refs, held_ref, held_sem = refs
    tiles_copy = pltpu.make_async_copy(refs[7], held_ref, held_sem)
    tiles_copy.start()
    tiles_copy.wait()
    lists = refs[:5]
    list_ref, more_ref, more_ids_ref, total_ref, ids_ref = lists
    mine_ref, other_ref, _, out_ref, acc_ref = refs[5:]
    tiles_ref = held_ref
    targets = out_ref.shape[0]

    def base(t, carry):
        product = grouped_product(tiles_ref, ids_ref, mine_ref, list_ref, t)
        product += grouped_product(tiles_ref, ids_ref, other_ref, list_ref, targets + t)
        acc_ref[t] = product
        out_ref[t] = product.astype(bf16)
        return carry

    lax.fori_loop(0, targets, base, 0, unroll=targets)

    def more(t, carry):
        target = more_ids_ref[t]
        place = target % targets

        @pl.when(target < targets)
        def _():
            acc_ref[place] += grouped_product(tiles_ref, ids_ref, mine_ref, more_ref, t)

        @pl.when(target >= targets)
        def _():
            acc_ref[place] += grouped_product(tiles_ref, ids_ref, other_ref, more_ref, t)

        out_ref[place] = acc_ref[place].astype(bf16)
        return carry

    lax.fori_loop(0, total_ref[0], more, 0)


def backward_tiles(lists, mine, other, tiles):
    width = mine.shape[-1]
    block = tiles.shape[-1]
    shape = (lists[0].shape[0] // (2 * quad), block, width)
    return pl.pallas_call(
        backward_kernel,
        out_shape=jax.ShapeDtypeStruct(shape, bf16),
        in_specs=[smem] * 5 + [vmem] * 2 + [pl.BlockSpec(memory_space=pltpu.HBM)],
        out_specs=vmem,
        scratch_shapes=[pltpu.VMEM(shape, f32), pltpu.VMEM(tiles.shape, bf16), pltpu.SemaphoreType.DMA],
        compiler_params=params(),
        cost_estimate=cost(4 * shape[0] * quad * block * block * width, tiles.size),
        name="backward_tiles",
    )(*lists, mine, other, pltpu.with_memory_space_constraint(tiles, pltpu.HBM))


def finish_kernel(upper_ref, parts_ref, weight_ref, held_ref, came_ref, out_ref, weight_out_ref):
    out_ref[...] = lax.dot_general(
        sum_parts(parts_ref).astype(bf16), weight_ref[...], (((1,), (1,)), ((), ())), preferred_element_type=f32
    ).astype(bf16)
    upper = upper_ref[0] == 1
    chunks, own, _ = held_ref.shape
    for k in range(2 * chunks):
        bits = [(k >> b) & 1 for b in range(3)]
        place = bits[1] * 2 + bits[2]
        held, came = held_ref[place], came_ref[place]
        low, high = (held, came) if bits[0] == 0 else (came, held)
        weight_out_ref[k * own : (k + 1) * own, :] = jnp.where(upper, high.astype(f32), low.astype(f32))


def finish(upper, parts, weight, held, came):
    return pl.pallas_call(
        finish_kernel,
        out_shape=(jax.ShapeDtypeStruct(parts.shape[1:], bf16), jax.ShapeDtypeStruct(weight.shape, f32)),
        in_specs=[smem] + [vmem] * 4,
        out_specs=(vmem,) * 2,
        compiler_params=params(),
        name="finish",
    )(upper, parts, weight, held, came)


def local(features, weight, block_values, block_rows, block_cols, counts, cotangent):
    rows_dev, width = features.shape
    row_count = lax.axis_size("row")
    col_count = lax.axis_size("col")
    node_total = rows_dev * row_count * col_count
    half = col_count // 2
    pairs = [(i, i ^ 1) for i in range(col_count)]
    groups = [[4 * y + 2 * x + c for x in range(2) for y in range(half // 2)] for c in range(2)]
    position = lax.axis_index("col").astype(i32)
    core = jnp.reshape(position % 2, (1,))
    tiles = block_values[0, 0]

    panel = lax.all_to_all(spread(features, row_count), "row", 0, 0)
    made = prepare(block_rows[0, 0], block_cols[0, 0], counts[0], core, tiles, col_count)
    forward_lists, (*backward_lists, backward_ids), flipped = made[:5], made[5:10], made[10]

    send = forward_tiles(1, forward_lists, panel, tiles)
    came = lax.ppermute(send, "col", pairs)
    keep = forward_tiles(0, forward_lists, panel, tiles)
    summed = (keep.astype(f32) + came.astype(f32)).astype(bf16)
    parts = lax.all_to_all(summed, "col", 0, 0, axis_index_groups=groups)
    activations, messages = dense(parts, weight, cotangent)

    mine = lax.all_to_all(messages, "col", 0, 0, axis_index_groups=groups)
    other = lax.ppermute(mine, "col", pairs)
    weight_rows, backward_ids = lax.optimization_barrier((weight_part(mine, row_count), backward_ids))
    weight_parts = lax.all_to_all(weight_rows, "row", 0, 0)
    back = backward_tiles((*backward_lists, backward_ids), mine, other, flipped)
    back_parts = lax.all_to_all(back, "row", 0, 0)
    weight_rows = weight_sum(weight_parts, 1.0 / math.sqrt(node_total))
    held, came = gather_over_col(weight_rows, position, col_count)
    upper = jnp.reshape((position // (col_count // 8)) % 2, (1,))
    feature_grad, weight_grad = finish(upper, back_parts, weight, held, came)
    return (activations, feature_grad, weight_grad)


def solution(mesh):
    in_specs = (
        P(("col", "row"), None),
        P(),
        P("row", "col", None, None, None),
        P("row", "col", None),
        P("row", "col", None),
        P("row", "col"),
        P(("row", "col"), None),
    )
    out_specs = (P(("row", "col"), None), P(("col", "row"), None), P())
    return jax.shard_map(local, mesh=mesh, in_specs=in_specs, out_specs=out_specs, check_vma=False)
```

```python
import functools
import math

import jax
import jax.numpy as jnp
from jax import lax
from jax.experimental import pallas as pl
from jax.experimental.pallas import tpu as pltpu
from jax.sharding import PartitionSpec as P

bf16 = jnp.bfloat16
f32 = jnp.float32
i32 = jnp.int32
smem = pl.BlockSpec(memory_space=pltpu.SMEM)
vmem = pl.BlockSpec(memory_space=pltpu.VMEM)
quad = 4


def params(mib=16):
    return pltpu.CompilerParams(vmem_limit_bytes=mib * 1024 * 1024)


def cost(flops, moved):
    return pl.CostEstimate(flops=flops, bytes_accessed=moved, transcendentals=0)


def sort_slots(target_of, slots, count, base_ref, extra_ref, extra_ids_ref, total_ref, seen_ref, last_ref):
    zero_slot = slots
    size = quad
    targets = base_ref.shape[0] // size

    def clear_base(t, carry):
        base_ref[t] = zero_slot
        return carry

    def clear_extra(t, carry):
        extra_ref[t] = zero_slot
        return carry

    def clear_seen(t, carry):
        seen_ref[t] = 0
        return carry

    lax.fori_loop(0, base_ref.shape[0], clear_base, 0)
    lax.fori_loop(0, extra_ref.shape[0], clear_extra, 0)
    lax.fori_loop(0, targets, clear_seen, 0)
    total_ref[0] = 0

    def place(s, carry):
        target = target_of(s)
        seen = seen_ref[target]
        seen_ref[target] = seen + 1

        @pl.when(seen < size)
        def _():
            base_ref[target * size + seen] = s

        @pl.when(seen >= size)
        def _():
            over = seen % size

            @pl.when(over == 0)
            def _():
                group = total_ref[0]
                total_ref[0] = group + 1
                last_ref[target] = group
                extra_ids_ref[group] = target

            extra_ref[last_ref[target] * size + over] = s

        return carry

    lax.fori_loop(0, count, place, 0)


def prepare_kernel(
    rows_ref, cols_ref, count_ref, core_ref, tiles_ref,
    fwd_ref, fwd_more_ref, fwd_more_ids_ref, fwd_total_ref, fwd_source_ref,
    bwd_ref, bwd_more_ref, bwd_more_ids_ref, bwd_total_ref, bwd_source_ref,
    flipped_ref, seen_ref, last_ref,
):
    slots = rows_ref.shape[0]
    count = count_ref[0]
    core = core_ref[0]
    half = fwd_ref.shape[0] // (2 * quad)

    def away(s):
        return (rows_ref[s] % 2 != core).astype(i32)

    def place(s):
        return (rows_ref[s] // 2 % 2) * (half // 2) + rows_ref[s] // 4

    def forward_target(s):
        return away(s) * half + place(s)

    def backward_target(s):
        return away(s) * half + cols_ref[s]

    sort_slots(forward_target, slots, count, fwd_ref, fwd_more_ref, fwd_more_ids_ref, fwd_total_ref, seen_ref, last_ref)
    sort_slots(backward_target, slots, count, bwd_ref, bwd_more_ref, bwd_more_ids_ref, bwd_total_ref, seen_ref, last_ref)

    def sources(s, carry):
        fwd_source_ref[s] = cols_ref[s]
        bwd_source_ref[s] = place(s)
        return carry

    lax.fori_loop(0, slots, sources, 0)
    fwd_source_ref[slots] = 0
    bwd_source_ref[slots] = 0

    def turn(s, carry):
        flipped_ref[s] = tiles_ref[s].T
        return carry

    lax.fori_loop(0, slots, turn, 0, unroll=4)
    flipped_ref[slots] = jnp.zeros(flipped_ref.shape[1:], bf16)


def prepare(rows_ids, cols_ids, count, core, tiles, targets):
    slots, block, _ = tiles.shape
    ints = lambda size: jax.ShapeDtypeStruct((size,), i32)
    held = jax.ShapeDtypeStruct((slots + 1, block, block), bf16)
    lists = (ints(targets * quad), ints(slots * quad), ints(slots), ints(1), ints(slots + 1))
    return pl.pallas_call(
        prepare_kernel,
        out_shape=(*lists, *lists, held),
        in_specs=[smem] * 4 + [vmem],
        out_specs=(smem,) * 10 + (vmem,),
        scratch_shapes=[pltpu.SMEM((targets,), i32)] * 2,
        compiler_params=params(24),
        cost_estimate=cost(0, 9 * slots * block * block * 2),
        name="prepare",
    )(rows_ids, cols_ids, count, core, tiles)


def grouped_product(tiles_ref, ids_ref, source_ref, list_ref, group):
    slots = [list_ref[group * quad + k] for k in range(quad)]
    block = tiles_ref.shape[1]
    held = tiles_ref.shape[0]
    if held == ids_ref.shape[0]:
        parts = [tiles_ref[s] for s in slots]
    else:
        parts = [tiles_ref[jnp.minimum(s, held - 1)] for s in slots]
        parts = [jnp.where(s < held, part, jnp.zeros_like(part)) for s, part in zip(slots, parts)]
    left = jnp.concatenate(parts, axis=1)
    right = jnp.concatenate([source_ref[ids_ref[s], :block, :] for s in slots], axis=0)
    return jnp.dot(left, right, preferred_element_type=f32)


def forward_kernel(part, *refs):
    lists = refs[:5]
    list_ref, more_ref, more_ids_ref, total_ref, ids_ref = lists
    panel_ref, tiles_ref, out_ref, acc_ref = refs[5:]
    half = out_ref.shape[0]

    def base(t, carry):
        product = grouped_product(tiles_ref, ids_ref, panel_ref, list_ref, part * half + t)
        acc_ref[t] = product
        out_ref[t] = product.astype(bf16)
        return carry

    lax.fori_loop(0, half, base, 0, unroll=half)

    def more(t, carry):
        place = more_ids_ref[t] - part * half

        @pl.when((place >= 0) & (place < half))
        def _():
            total = acc_ref[place] + grouped_product(tiles_ref, ids_ref, panel_ref, more_ref, t)
            acc_ref[place] = total
            out_ref[place] = total.astype(bf16)

        return carry

    lax.fori_loop(0, total_ref[0], more, 0)


def forward_tiles(part, lists, panel, tiles):
    block, width = panel.shape[1:]
    shape = (lists[0].shape[0] // (2 * quad), block, width)
    return pl.pallas_call(
        functools.partial(forward_kernel, part),
        out_shape=jax.ShapeDtypeStruct(shape, bf16),
        in_specs=[smem] * 5 + [vmem] * 2,
        out_specs=vmem,
        scratch_shapes=[pltpu.VMEM(shape, f32)],
        compiler_params=params(),
        cost_estimate=cost(2 * shape[0] * quad * block * block * width, tiles.size),
        name="forward_tiles_%d" % part,
    )(*lists, panel, tiles)


def spread_kernel(in_ref, out_ref):
    for k in range(out_ref.shape[0]):
        out_ref[k] = in_ref[...]


def spread(shard, copies):
    return pl.pallas_call(
        spread_kernel,
        out_shape=pltpu.VMEM((copies,) + shard.shape, shard.dtype),
        in_specs=[vmem],
        out_specs=vmem,
        compiler_params=params(),
        name="spread",
    )(shard)


def sum_parts(ref):
    total = ref[0].astype(f32)
    for k in range(1, ref.shape[0]):
        total += ref[k].astype(f32)
    return total


def dense_kernel(parts_ref, weight_ref, cotangent_ref, act_ref, message_ref):
    aggregated = sum_parts(parts_ref)
    aggregated_half = aggregated.astype(bf16)
    preact = jnp.dot(aggregated_half, weight_ref[...], preferred_element_type=f32)
    scale = math.sqrt(2 / math.pi)
    square = preact * preact
    tanh = jnp.tanh(scale * (preact + 0.044715 * (square * preact)))
    act_ref[...] = (0.5 * preact * (1.0 + tanh)).astype(bf16)
    slope = 0.5 * (1.0 + tanh) + (0.5 * preact) * (1.0 - tanh * tanh) * (
        scale * (1.0 + (3 * 0.044715) * square)
    )
    grad_pre = (cotangent_ref[...].astype(f32) * slope).astype(bf16)
    turned = aggregated_half.astype(f32).T
    peers = message_ref.shape[0]
    rows = grad_pre.shape[0]
    own = 2 * turned.shape[0] // peers
    for k in range(peers):
        message_ref[k, :rows, :] = grad_pre
        first = (k % (peers // 2)) * own
        low = turned[first : first + own // 2]
        high = turned[first + own // 2 : first + own]
        message_ref[k, rows:, :] = jnp.concatenate([low, high], axis=1).astype(bf16)


def dense(parts, weight, cotangent):
    rows, width = cotangent.shape
    peers = parts.shape[0]
    return pl.pallas_call(
        dense_kernel,
        out_shape=(
            jax.ShapeDtypeStruct((rows, width), bf16),
            jax.ShapeDtypeStruct((peers, rows + width // peers, width), bf16),
        ),
        in_specs=[vmem] * 3,
        out_specs=(vmem,) * 2,
        compiler_params=params(),
        name="dense",
    )(parts, weight, cotangent)


def weight_kernel(mine_ref, out_ref):
    peers, _, width = mine_ref.shape
    rows = width // 2
    total = None
    for k in range(0, peers, 2):
        left = []
        for p in (k, k + 1):
            packed = mine_ref[p, rows:, :].astype(f32)
            left.append(jnp.concatenate([packed[:, :rows], packed[:, rows:]], axis=0))
        left = jnp.concatenate(left, axis=1).astype(bf16)
        right = jnp.concatenate([mine_ref[k, :rows, :], mine_ref[k + 1, :rows, :]], axis=0)
        term = jnp.dot(left, right, preferred_element_type=f32)
        total = term if total is None else total + term
    rounded = total.astype(bf16)
    for k in range(out_ref.shape[0]):
        out_ref[k] = rounded


def weight_part(mine, copies):
    peers, _, width = mine.shape
    return pl.pallas_call(
        weight_kernel,
        out_shape=jax.ShapeDtypeStruct((copies, 2 * width // peers, width), bf16),
        in_specs=[vmem],
        out_specs=vmem,
        compiler_params=params(),
        cost_estimate=cost(0, mine.size),
        name="weight_part",
    )(mine)


def weight_sum_kernel(scale, parts_ref, out_ref):
    out_ref[...] = sum_parts(parts_ref) * scale


def weight_sum(parts, scale):
    return pl.pallas_call(
        functools.partial(weight_sum_kernel, scale),
        out_shape=jax.ShapeDtypeStruct(parts.shape[1:], f32),
        in_specs=[vmem],
        out_specs=vmem,
        compiler_params=params(),
        cost_estimate=cost(0, parts.size),
        name="weight_sum",
    )(parts)


def gather_over_col(rows, position, size):
    held = (rows + lax.ppermute(rows, "col", [(i, i ^ 1) for i in range(size)]))[None]
    steps = (size // 8, size // 4, size // 2)
    for distance in steps:
        came = lax.ppermute(held, "col", [(i, i ^ distance) for i in range(size)])
        if distance == steps[-1]:
            return held, came
        upper = (position // distance) % 2 == 1
        held = jnp.where(upper, jnp.concatenate([came, held]), jnp.concatenate([held, came]))


def backward_kernel(*refs):
    *refs, held_ref, held_sem = refs
    tiles_copy = pltpu.make_async_copy(refs[7], held_ref, held_sem)
    tiles_copy.start()
    tiles_copy.wait()
    lists = refs[:5]
    list_ref, more_ref, more_ids_ref, total_ref, ids_ref = lists
    mine_ref, other_ref, _, out_ref, acc_ref = refs[5:]
    tiles_ref = held_ref
    targets = out_ref.shape[0]

    def base(t, carry):
        product = grouped_product(tiles_ref, ids_ref, mine_ref, list_ref, t)
        product += grouped_product(tiles_ref, ids_ref, other_ref, list_ref, targets + t)
        acc_ref[t] = product
        out_ref[t] = product.astype(bf16)
        return carry

    lax.fori_loop(0, targets, base, 0, unroll=targets)

    def more(t, carry):
        target = more_ids_ref[t]
        place = target % targets

        @pl.when(target < targets)
        def _():
            acc_ref[place] += grouped_product(tiles_ref, ids_ref, mine_ref, more_ref, t)

        @pl.when(target >= targets)
        def _():
            acc_ref[place] += grouped_product(tiles_ref, ids_ref, other_ref, more_ref, t)

        out_ref[place] = acc_ref[place].astype(bf16)
        return carry

    lax.fori_loop(0, total_ref[0], more, 0)


def backward_tiles(lists, mine, other, tiles):
    width = mine.shape[-1]
    block = tiles.shape[-1]
    shape = (lists[0].shape[0] // (2 * quad), block, width)
    return pl.pallas_call(
        backward_kernel,
        out_shape=jax.ShapeDtypeStruct(shape, bf16),
        in_specs=[smem] * 5 + [vmem] * 2 + [pl.BlockSpec(memory_space=pltpu.HBM)],
        out_specs=vmem,
        scratch_shapes=[pltpu.VMEM(shape, f32), pltpu.VMEM(tiles.shape, bf16), pltpu.SemaphoreType.DMA],
        compiler_params=params(),
        cost_estimate=cost(4 * shape[0] * quad * block * block * width, tiles.size),
        name="backward_tiles",
    )(*lists, mine, other, pltpu.with_memory_space_constraint(tiles, pltpu.HBM))


def finish_kernel(upper_ref, parts_ref, weight_ref, held_ref, came_ref, out_ref, weight_out_ref):
    out_ref[...] = lax.dot_general(
        sum_parts(parts_ref).astype(bf16), weight_ref[...], (((1,), (1,)), ((), ())), preferred_element_type=f32
    ).astype(bf16)
    upper = upper_ref[0] == 1
    chunks, own, _ = held_ref.shape
    for k in range(2 * chunks):
        bits = [(k >> b) & 1 for b in range(3)]
        place = bits[1] * 2 + bits[0]
        held, came = held_ref[place], came_ref[place]
        low, high = (held, came) if bits[2] == 0 else (came, held)
        weight_out_ref[k * own : (k + 1) * own, :] = jnp.where(upper, high, low)


def finish(upper, parts, weight, held, came):
    return pl.pallas_call(
        finish_kernel,
        out_shape=(jax.ShapeDtypeStruct(parts.shape[1:], bf16), jax.ShapeDtypeStruct(weight.shape, f32)),
        in_specs=[smem] + [vmem] * 4,
        out_specs=(vmem,) * 2,
        compiler_params=params(),
        name="finish",
    )(upper, parts, weight, held, came)


def local(features, weight, block_values, block_rows, block_cols, counts, cotangent):
    rows_dev, width = features.shape
    row_count = lax.axis_size("row")
    col_count = lax.axis_size("col")
    node_total = rows_dev * row_count * col_count
    half = col_count // 2
    pairs = [(i, i ^ 1) for i in range(col_count)]
    groups = [[4 * y + 2 * x + c for x in range(2) for y in range(half // 2)] for c in range(2)]
    position = lax.axis_index("col").astype(i32)
    core = jnp.reshape(position % 2, (1,))
    tiles = block_values[0, 0]

    panel = lax.all_to_all(spread(features, row_count), "row", 0, 0)
    made = prepare(block_rows[0, 0], block_cols[0, 0], counts[0], core, tiles, col_count)
    forward_lists, (*backward_lists, backward_ids), flipped = made[:5], made[5:10], made[10]

    send = forward_tiles(1, forward_lists, panel, tiles)
    came = lax.ppermute(send, "col", pairs)
    keep = forward_tiles(0, forward_lists, panel, tiles)
    summed = (keep.astype(f32) + came.astype(f32)).astype(bf16)
    parts = lax.all_to_all(summed, "col", 0, 0, axis_index_groups=groups)
    activations, messages = dense(parts, weight, cotangent)

    mine = lax.all_to_all(messages, "col", 0, 0, axis_index_groups=groups)
    other = lax.ppermute(mine, "col", pairs)
    weight_rows, backward_ids = lax.optimization_barrier((weight_part(mine, row_count), backward_ids))
    weight_parts = lax.all_to_all(weight_rows, "row", 0, 0)
    back = backward_tiles((*backward_lists, backward_ids), mine, other, flipped)
    back_parts = lax.all_to_all(back, "row", 0, 0)
    weight_rows = weight_sum(weight_parts, 1.0 / math.sqrt(node_total))
    held, came = gather_over_col(weight_rows, position, col_count)
    upper = jnp.reshape((position // (col_count // 2)) % 2, (1,))
    feature_grad, weight_grad = finish(upper, back_parts, weight, held, came)
    return (activations, feature_grad, weight_grad)


def solution(mesh):
    in_specs = (
        P(("col", "row"), None),
        P(),
        P("row", "col", None, None, None),
        P("row", "col", None),
        P("row", "col", None),
        P("row", "col"),
        P(("row", "col"), None),
    )
    out_specs = (P(("row", "col"), None), P(("col", "row"), None), P())
    return jax.shard_map(local, mesh=mesh, in_specs=in_specs, out_specs=out_specs, check_vma=False)
```
